32 devices in a mesh: ctx: 8 (over y, x, core), fsdp: 4 (over z).
Axes of the slice: x: 2, y: 2, z: 4, core: 2. Of those that a mesh axis runs over, the one named last changes fastest.
Arguments:
- tokens: bfloat16 [4, 1024, 2304], P('fsdp', 'ctx'), may hold values from -6 to 6
- cotangent: bfloat16 [4, 1024, 2304], P('fsdp', 'ctx'), may hold values from -6 to 6
- block_order: int32 [16], replicated, may hold values from 0 to 15, each once
- w_qkv: float32 [2304, 4096], P(('ctx', 'fsdp')), may hold values from -0.125 to 0.125
- w_out: float32 [2304, 2048], P(('ctx', 'fsdp')), may hold values from -0.125 to 0.125
- w_gate_up: float32 [2304, 18432], P(('ctx', 'fsdp')), may hold values from -0.125 to 0.125
- w_down: float32 [2304, 9216], P(('ctx', 'fsdp')), may hold values from -0.0625 to 0.0625
- norm_gains: float32 [4, 2304], P(None, ('ctx', 'fsdp')), may hold values from 0.5 to 1.5
- first_qkv: float32 [2304, 4096], P(('ctx', 'fsdp')), may hold values from -20 to 20
- first_out: float32 [2304, 2048], P(('ctx', 'fsdp')), may hold values from -40 to 40
- first_gate_up: float32 [2304, 18432], P(('ctx', 'fsdp')), may hold values from -20 to 20
- first_down: float32 [2304, 9216], P(('ctx', 'fsdp')), may hold values from -40 to 40
- first_gains: float32 [4, 2304], P(None, ('ctx', 'fsdp')), may hold values from -40 to 40
- second_qkv: float32 [2304, 4096], P(('ctx', 'fsdp')), may hold values from 27.0336 to 430.08
- second_out: float32 [2304, 2048], P(('ctx', 'fsdp')), may hold values from 106.496 to 1720.32
- second_gate_up: float32 [2304, 18432], P(('ctx', 'fsdp')), may hold values from 27.0336 to 430.08
- second_down: float32 [2304, 9216], P(('ctx', 'fsdp')), may hold values from 106.496 to 1720.32
- second_gains: float32 [4, 2304], P(None, ('ctx', 'fsdp')), may hold values from 106.496 to 1720.32
Outputs:
- output: bfloat16 [4, 1024, 2304], P('fsdp', 'ctx')
- token_grad: bfloat16 [4, 1024, 2304], P('fsdp', 'ctx')
- moment_qkv: float32 [2304, 4096], P(('ctx', 'fsdp'))
- moment_out: float32 [2304, 2048], P(('ctx', 'fsdp'))
- moment_gate_up: float32 [2304, 18432], P(('ctx', 'fsdp'))
- moment_down: float32 [2304, 9216], P(('ctx', 'fsdp'))
- moment_gains: float32 [4, 2304], P(None, ('ctx', 'fsdp'))
- square_qkv: float32 [2304, 4096], P(('ctx', 'fsdp'))
- square_out: float32 [2304, 2048], P(('ctx', 'fsdp'))
- square_gate_up: float32 [2304, 18432], P(('ctx', 'fsdp'))
- square_down: float32 [2304, 9216], P(('ctx', 'fsdp'))
- square_gains: float32 [4, 2304], P(None, ('ctx', 'fsdp'))
- new_qkv: float32 [2304, 4096], P(('ctx', 'fsdp'))
- new_out: float32 [2304, 2048], P(('ctx', 'fsdp'))
- new_gate_up: float32 [2304, 18432], P(('ctx', 'fsdp'))
- new_down: float32 [2304, 9216], P(('ctx', 'fsdp'))
- new_gains: float32 [4, 2304], P(None, ('ctx', 'fsdp'))
The draws below stay inside these ranges and needn't reach their ends.
Inputs may be any that keep to these rules, and one draw needn't show every extreme that they name: Slot s of every sequence holds that sequence's block number block_order[s]; each block number appears once.
All inputs are finite; a program needn't handle non-finite values.
Results may differ from the reference program's by a relative error of at most 0.025.
Values may be sent and summed in bfloat16 or wider, within the bound.
No kernel may reach another device: no remote copies, remote signals or barrier semaphores. Data moves between devices by JAX's collectives and lax.ppermute only.
A program may use at most 512 MiB of HBM per device.

```python
import math
import jax
import jax.numpy as jnp
from jax import lax

D = 2304
FF = 9216
HEADS = 8
KV_HEADS = 4
HEAD_DIM = 256
BLOCK = 64
STEP = 5
Q_WIDTH = 2048
KV_WIDTH = 1024
LENGTH = 1024
SEQS = 4
TOKENS = 4096
N_CTX = 8


def raised(drawn, rng, source, target, shards_of, factor):
    def block_of(position):
        return (jnp.arange(drawn.shape[position]) // (drawn.shape[position] // shards_of)).reshape((-1,) + (1,) * (drawn.ndim - 1 - position))

    one_side = jax.random.permutation(rng, shards_of)[block_of(target)]
    second = (block_of(target) + shards_of // 2) % shards_of
    return jnp.where((block_of(source) == one_side) | (block_of(source) == second), factor * drawn, drawn)


def shard_levels(rng, extent, cuts, low, top_value):
    def one(position, parts):
        steps = jax.random.uniform(jax.random.fold_in(jax.random.fold_in(rng, 6), position), (parts,), jnp.float32, low / len(cuts), top_value / len(cuts))
        return jnp.repeat(jnp.exp(steps), extent[position] // parts).reshape((-1,) + (1,) * (len(extent) - position - 1))

    loudness = one(*cuts[0])
    for cut in cuts[1:]:
        loudness = loudness * one(*cut)
    return loudness


def bell_draw(stream_key, shape, width, most, cuts=(), kind=jnp.bfloat16):
    values = width * jax.random.normal(stream_key, shape, jnp.float32)
    if cuts:
        values = values * shard_levels(stream_key, shape, cuts, -0.22, 0.18)
    return jnp.clip(values, -most, most).astype(kind)


def noise_with(rng, shape, spread, limit, shards, heavy, held_as=jnp.bfloat16):
    array = spread * jax.random.normal(rng, shape, jnp.float32)
    if shards:
        array = array * shard_levels(rng, shape, shards, -0.22, 0.18)
    return jnp.clip(raised(array, jax.random.fold_in(rng, 3), *heavy), -limit, limit).astype(held_as)


def setup_inputs(seed: int = 0) -> dict:
    key_list = jax.random.split(jax.random.key(seed), 19)
    tokens = bell_draw(key_list[0], (SEQS, LENGTH, D), 1.0, 6.0, ((0, 4), (1, 8)))
    cotangent = noise_with(key_list[1], (SEQS, LENGTH, D), 1.0, 6.0, ((0, 4), (1, 8)), (1, 2, 8, 2.0))
    block_order = jax.random.permutation(key_list[2], 2 * N_CTX).astype(jnp.int32)
    w_qkv = bell_draw(key_list[3], (D, Q_WIDTH + 2 * KV_WIDTH), D ** -0.5, 0.125, ((0, 32),), jnp.float32)
    w_out = bell_draw(key_list[4], (D, Q_WIDTH), Q_WIDTH ** -0.5, 0.125, ((0, 32),), jnp.float32)
    w_gate_up = bell_draw(key_list[5], (D, 2 * FF), D ** -0.5, 0.125, ((0, 32),), jnp.float32)
    w_down = bell_draw(key_list[6], (D, FF), FF ** -0.5, 0.0625, ((0, 32),), jnp.float32)
    norm_gains = jnp.clip(1.0 + 0.1 * jax.random.normal(key_list[7], (4, D), jnp.float32), 0.5, 1.5)
    first_qkv = bell_draw(key_list[8], (D, Q_WIDTH + 2 * KV_WIDTH), (0.055 * TOKENS ** 0.5), 20.0, ((0, 32),), jnp.float32)
    first_out = bell_draw(key_list[9], (D, Q_WIDTH), (0.11 * TOKENS ** 0.5), 40.0, ((0, 32),), jnp.float32)
    first_gate_up = bell_draw(key_list[10], (D, 2 * FF), (0.055 * TOKENS ** 0.5), 20.0, ((0, 32),), jnp.float32)
    first_down = bell_draw(key_list[11], (D, FF), (0.11 * TOKENS ** 0.5), 40.0, ((0, 32),), jnp.float32)
    first_gains = bell_draw(key_list[12], (4, D), (0.11 * TOKENS ** 0.5), 40.0, ((1, 32),), jnp.float32)
    second_qkv = jnp.clip(jnp.exp(math.log(430.08) - 2.7668907 * jax.random.uniform(key_list[13], (D, Q_WIDTH + 2 * KV_WIDTH), jnp.float32) ** shard_levels(key_list[13], (D, Q_WIDTH + 2 * KV_WIDTH), ((0, 32),), -0.2, 0.2)), 27.0336, 430.08)
    second_out = jnp.clip(jnp.exp(math.log(1720.32) - 2.7821581 * jax.random.uniform(key_list[14], (D, Q_WIDTH), jnp.float32) ** shard_levels(key_list[14], (D, Q_WIDTH), ((0, 32),), -0.2, 0.2)), 106.496, 1720.32)
    second_gate_up = jnp.clip(jnp.exp(math.log(430.08) - 2.7668907 * jax.random.uniform(key_list[15], (D, 2 * FF), jnp.float32) ** shard_levels(key_list[15], (D, 2 * FF), ((0, 32),), -0.2, 0.2)), 27.0336, 430.08)
    second_down = jnp.clip(jnp.exp(math.log(1720.32) - 2.7821581 * jax.random.uniform(key_list[16], (D, FF), jnp.float32) ** shard_levels(key_list[16], (D, FF), ((0, 32),), -0.2, 0.2)), 106.496, 1720.32)
    second_gains = jnp.clip(jnp.exp(math.log(1720.32) - 2.7821581 * jax.random.uniform(key_list[17], (4, D), jnp.float32) ** shard_levels(key_list[17], (4, D), ((1, 32),), -0.2, 0.2)), 106.496, 1720.32)
    return dict(tokens=tokens, cotangent=cotangent, block_order=block_order, w_qkv=w_qkv, w_out=w_out, w_gate_up=w_gate_up, w_down=w_down, norm_gains=norm_gains, first_qkv=first_qkv, first_out=first_out, first_gate_up=first_gate_up, first_down=first_down, first_gains=first_gains, second_qkv=second_qkv, second_out=second_out, second_gate_up=second_gate_up, second_down=second_down, second_gains=second_gains)


SOFT_CAP = 3.0
NORM_EPS = 1e-06
BETA_ONE = 0.9
BETA_TWO = 0.95
ADAM_EPS = 1e-08
MATRIX_RATE = 0.02
GAIN_RATE = 0.3
WEIGHT_DECAY = 0.1
HIGHEST = lax.Precision.HIGHEST

@jax.custom_vjp
def low(v):
    return lax.optimization_barrier(v.astype(jnp.bfloat16)).astype(jnp.float32)

@jax.custom_vjp
def low_back(v):
    return v

def low_keep(v):
    return (low(v), None)

def low_pass(kept, grad):
    return (grad,)

def back_keep(v):
    return (v, None)

def back_low(kept, grad):
    return (low(grad),)
low.defvjp(low_keep, low_pass)
low_back.defvjp(back_keep, back_low)

def rms_norm(values, gain_row):
    return values * lax.rsqrt(lax.optimization_barrier(jnp.mean(values * values, -1, keepdims=True)) + NORM_EPS) * gain_row

def gelu_tanh(values):
    return 0.5 * values * (1.0 + jnp.tanh(0.7978845608028654 * (values + 0.044715 * values * values * values)))

def rotate(values, cos_table, sin_table):
    half_dim = values.shape[-1] // 2
    front_half = values[..., :half_dim]
    back_half = values[..., half_dim:]
    return jnp.concatenate([front_half * cos_table - back_half * sin_table, back_half * cos_table + front_half * sin_table], -1)

def rope_tables(positions):
    frequency = 10000.0 ** (-(jnp.arange(HEAD_DIM // 2, dtype=jnp.float32) * 2.0) / HEAD_DIM)
    turned = positions.astype(jnp.float32)[:, None] * frequency[None, :]
    return (jnp.cos(turned)[:, None, :], jnp.sin(turned)[:, None, :])

def adamw(weight, moment_one, moment_two, gradient, rate, decay):
    first_new = BETA_ONE * moment_one + (1.0 - BETA_ONE) * gradient
    second_new = BETA_TWO * moment_two + (1.0 - BETA_TWO) * gradient * gradient
    step_size = first_new / (1.0 - BETA_ONE ** STEP) / (jnp.sqrt(second_new / (1.0 - BETA_TWO ** STEP)) + ADAM_EPS)
    return (first_new, second_new, weight - rate * (step_size + decay * weight))

def layer_forward(token_rows, w_qkv, w_out, w_gate_up, w_down, gains, cos_table, sin_table, allowed):
    q_width = HEADS * HEAD_DIM
    kv_width = KV_HEADS * HEAD_DIM
    group_size = HEADS // KV_HEADS
    scale = HEAD_DIM ** (-0.5)
    normed_one = low(rms_norm(token_rows, gains[0]))
    projected = low_back(jnp.dot(normed_one, w_qkv, precision=HIGHEST, preferred_element_type=jnp.float32))
    queries = low(rotate(projected[:, :q_width].reshape(LENGTH, HEADS, HEAD_DIM), cos_table, sin_table))
    keys_roped = low(rotate(projected[:, q_width:q_width + kv_width].reshape(LENGTH, KV_HEADS, HEAD_DIM), cos_table, sin_table))
    values_low = low(projected[:, q_width + kv_width:].reshape(LENGTH, KV_HEADS, HEAD_DIM))
    grouped = queries.reshape(LENGTH, KV_HEADS, group_size, HEAD_DIM)
    raw_scores = low_back(jnp.einsum('qkgd,pkd->kgqp', grouped, keys_roped, precision=HIGHEST) * scale)
    capped = jnp.where(allowed, SOFT_CAP * jnp.tanh(raw_scores / SOFT_CAP), -1e+30)
    top_score = lax.optimization_barrier(jnp.max(capped, -1, keepdims=True))
    exp_scores = jnp.exp(capped - top_score)
    attn_probs = low(exp_scores / lax.optimization_barrier(jnp.sum(exp_scores, -1, keepdims=True)))
    attended = jnp.einsum('kgqp,pkd->qkgd', attn_probs, values_low, precision=HIGHEST).reshape(LENGTH, q_width)
    attended = low_back(low(attended))
    branch = low_back(jnp.einsum('th,dh->td', attended, w_out, precision=HIGHEST))
    hidden_in = token_rows + rms_norm(branch, gains[1])
    normed_two = low(rms_norm(hidden_in, gains[2]))
    gate_up = low_back(jnp.dot(normed_two, w_gate_up, precision=HIGHEST, preferred_element_type=jnp.float32))
    activated = low(gelu_tanh(gate_up[:, :FF]) * gate_up[:, FF:])
    lowered = low_back(jnp.einsum('tf,df->td', activated, w_down, precision=HIGHEST))
    return hidden_in + rms_norm(lowered, gains[3])

def reference(tokens, cotangent, block_order, w_qkv, w_out, w_gate_up, w_down, norm_gains, first_qkv, first_out, first_gate_up, first_down, first_gains, second_qkv, second_out, second_gate_up, second_down, second_gains):
    row_ids = jnp.arange(LENGTH, dtype=jnp.int32)
    positions = block_order[row_ids // BLOCK].astype(jnp.int32) * BLOCK + row_ids % BLOCK
    cos_table, sin_table = rope_tables(positions)
    allowed = positions[None, :] <= positions[:, None]

    def forward(sequence_rows, qkv_master, out_master, gate_up_master, down_master, gain_master):
        qkv_low = low(qkv_master)
        out_low = low(out_master)
        gate_up_low = low(gate_up_master)
        down_low = low(down_master)
        gains_low = low(gain_master)

        def one_sequence(carry_dummy, token_rows):
            return (carry_dummy, layer_forward(token_rows, qkv_low, out_low, gate_up_low, down_low, gains_low, cos_table, sin_table, allowed))
        _, outputs = lax.scan(jax.checkpoint(one_sequence), jnp.zeros((), jnp.float32), sequence_rows)
        return outputs
    outputs, pull_back = jax.vjp(forward, tokens.astype(jnp.float32), w_qkv, w_out, w_gate_up, w_down, norm_gains)
    token_grads, grad_qkv, grad_out, grad_gate_up, grad_down, grad_gains = pull_back(cotangent.astype(jnp.float32))
    moment_qkv, square_qkv, new_qkv = adamw(w_qkv, first_qkv, second_qkv, grad_qkv, MATRIX_RATE, WEIGHT_DECAY)
    moment_out, square_out, new_out = adamw(w_out, first_out, second_out, grad_out, MATRIX_RATE, WEIGHT_DECAY)
    moment_gate_up, square_gate_up, new_gate_up = adamw(w_gate_up, first_gate_up, second_gate_up, grad_gate_up, MATRIX_RATE, WEIGHT_DECAY)
    moment_down, square_down, new_down = adamw(w_down, first_down, second_down, grad_down, MATRIX_RATE, WEIGHT_DECAY)
    moment_gains, square_gains, new_gains = adamw(norm_gains, first_gains, second_gains, grad_gains, GAIN_RATE, 0.0)
    return (outputs.astype(jnp.bfloat16), token_grads.astype(jnp.bfloat16), moment_qkv, moment_out, moment_gate_up, moment_down, moment_gains, square_qkv, square_out, square_gate_up, square_down, square_gains, new_qkv, new_out, new_gate_up, new_down, new_gains)
```

```python
import jax
import jax.numpy as jnp
from jax import lax
from jax.sharding import Mesh
from jax.sharding import PartitionSpec as P

HEADS = 8
KV_HEADS = 4
HEAD_DIM = 256
STEP = 5


SOFT_CAP = 3.0
NORM_EPS = 1e-06
BETA_ONE = 0.9
BETA_TWO = 0.95
ADAM_EPS = 1e-08
MATRIX_RATE = 0.02
GAIN_RATE = 0.3
WEIGHT_DECAY = 0.1

PLANE = ("y", "x")
HEAD_AXES = ("y", "x", "core")
CTX = ("row", "y", "x", "core")
TENSOR = ("core", "fsdp")
EVERY = ("row", "y", "x", "core", "fsdp")


def rms_norm(values, gain_row):
    return values * lax.rsqrt(jnp.mean(values * values, -1, keepdims=True) + NORM_EPS) * gain_row


def norm_back(values, gain_row, grad_out):
    _, pull_back = jax.vjp(rms_norm, values, gain_row)
    grad_values, grad_gain = pull_back(grad_out)
    return (grad_values, jnp.sum(grad_gain.reshape(-1, grad_gain.shape[-1]), 0))


def gelu_tanh(values):
    return (
        0.5
        * values
        * (1.0 + jnp.tanh(0.7978845608028654 * (values + 0.044715 * values * values * values)))
    )


def gated_unit(gate_part, up_part):
    return gelu_tanh(gate_part) * up_part


def rotate(values, cos_table, sin_table):
    half_dim = values.shape[-1] // 2
    front_half = values[..., :half_dim]
    back_half = values[..., half_dim:]
    return jnp.concatenate(
        [
            front_half * cos_table - back_half * sin_table,
            back_half * cos_table + front_half * sin_table,
        ],
        -1,
    )


def rope_tables(positions, head_size):
    frequency = 10000.0 ** (-(jnp.arange(head_size // 2, dtype=jnp.float32) * 2.0) / head_size)
    turned = positions.astype(jnp.float32)[:, None] * frequency[None, :]
    return (jnp.cos(turned), jnp.sin(turned))


def positions_of(slot_table, row_total, block_size):
    row_ids = jnp.arange(row_total, dtype=jnp.int32)
    slot_ids = row_ids // block_size
    picked = jnp.sum(
        jnp.where(
            slot_ids[:, None] == jnp.arange(slot_table.shape[0], dtype=jnp.int32)[None, :],
            slot_table[None, :],
            0,
        ),
        1,
    )
    return picked * block_size + row_ids % block_size


def adamw(weight, moment_one, moment_two, gradient, rate, decay):
    first_new = BETA_ONE * moment_one + (1.0 - BETA_ONE) * gradient
    second_new = BETA_TWO * moment_two + (1.0 - BETA_TWO) * gradient * gradient
    step_size = (
        first_new
        / (1.0 - BETA_ONE**STEP)
        / (jnp.sqrt(second_new / (1.0 - BETA_TWO**STEP)) + ADAM_EPS)
    )
    return (first_new, second_new, weight - rate * (step_size + decay * weight))


def low(values):
    return values.astype(jnp.bfloat16)


def dot(left, right):
    return jnp.dot(left, right, preferred_element_type=jnp.float32)


def dot_t(left, right):
    return lax.dot_general(left, right, (((1,), (1,)), ((), ())), preferred_element_type=jnp.float32)


def t_dot(left, right):
    return lax.dot_general(left, right, (((0,), (0,)), ((), ())), preferred_element_type=jnp.float32)


def gather_rows(piece, axes):
    return lax.all_gather(piece, axes, axis=0, tiled=True)


def scatter_rows(terms, axes):
    return lax.psum_scatter(terms, axes, scatter_dimension=0, tiled=True)


def exchange(piece, axis):
    return lax.ppermute(piece, axis, [(0, 1), (1, 0)])


def columns_out(weight_piece, axes, parts):
    rows = weight_piece.shape[0]
    blocks = weight_piece.reshape(rows, parts, -1)
    return lax.all_to_all(blocks, axes, split_axis=1, concat_axis=0, tiled=True).reshape(
        parts * rows, -1
    )


def columns_back(grad_piece, axes, parts):
    rows = grad_piece.shape[0] // parts
    blocks = grad_piece.reshape(parts, rows, -1)
    return jnp.transpose(
        lax.all_to_all(blocks, axes, split_axis=0, concat_axis=0, tiled=True), (1, 0, 2)
    )


def per_device(
    tokens,
    cotangent,
    block_order,
    w_qkv,
    w_out,
    w_gate_up,
    w_down,
    norm_gains,
    first_qkv,
    first_out,
    first_gate_up,
    first_down,
    first_gains,
    second_qkv,
    second_out,
    second_gate_up,
    second_down,
    second_gains,
):
    row_count = tokens.shape[1]
    block_size = row_count // 2
    row_parts = lax.axis_size("row")
    fsdp_count = lax.axis_size("fsdp")
    core_id = lax.axis_index("core")
    row_id = lax.axis_index("row")
    seq_length = row_count * row_parts * HEADS
    query_rows = row_count * HEADS
    own_rows = w_qkv.shape[0]
    width = tokens.shape[2]
    q_width = HEADS * HEAD_DIM
    kv_width = KV_HEADS * HEAD_DIM
    ff_width = w_down.shape[1]
    tensor_parts = 2 * fsdp_count
    ff_own = ff_width // tensor_parts
    scale = HEAD_DIM ** (-0.5)

    q_cols = low(w_qkv[:, :q_width]).reshape(own_rows, HEADS, HEAD_DIM)
    k_cols = low(w_qkv[:, q_width : q_width + kv_width]).reshape(own_rows, KV_HEADS, 1, HEAD_DIM)
    v_cols = low(w_qkv[:, q_width + kv_width :]).reshape(own_rows, KV_HEADS, 1, HEAD_DIM)
    kv_cols = jnp.concatenate([k_cols, v_cols], 2).reshape(own_rows, HEADS, HEAD_DIM)

    def head_weight(cols):
        mine = columns_out(cols, HEAD_AXES, HEADS).reshape(HEADS, own_rows, -1)
        every = lax.all_gather(mine, "fsdp", axis=1, tiled=False)
        if row_parts > 1:
            every = lax.all_gather(every, "row", axis=0, tiled=True)
        return every.reshape(width, -1)

    head_qkv = head_weight(jnp.concatenate([q_cols, kv_cols], 2))
    head_out = head_weight(low(w_out).reshape(own_rows, HEADS, HEAD_DIM))

    gate_up_cols = jnp.concatenate(
        [
            low(w_gate_up[:, :ff_width]).reshape(own_rows, tensor_parts, ff_own),
            low(w_gate_up[:, ff_width:]).reshape(own_rows, tensor_parts, ff_own),
        ],
        2,
    )
    own_gate_up = gather_rows(
        columns_out(gate_up_cols, TENSOR, tensor_parts), ("row",) + PLANE
    )
    own_down = gather_rows(
        columns_out(low(w_down), TENSOR, tensor_parts), ("row",) + PLANE
    )

    gains = lax.all_gather(low(norm_gains), EVERY, axis=1, tiled=True).astype(jnp.float32)

    key_positions = positions_of(block_order, seq_length, block_size)
    cos_table, sin_table = rope_tables(key_positions, HEAD_DIM)
    first_row = row_id * query_rows

    def query_part(array):
        if row_parts == 1:
            return array
        return lax.dynamic_slice_in_dim(array, first_row, query_rows, 0)

    query_cos, query_sin = query_part(cos_table), query_part(sin_table)
    allowed = key_positions[None, :] <= query_part(key_positions)[:, None]

    inputs = tokens[0].astype(jnp.float32)
    seq_tokens = gather_rows(tokens[0], CTX)
    normed_one = low(rms_norm(seq_tokens.astype(jnp.float32), gains[0]))
    normed_query = query_part(normed_one)
    queries = low(rotate(dot(normed_query, head_qkv[:, :HEAD_DIM]), query_cos, query_sin))
    kv_raw = dot(normed_one, head_qkv[:, HEAD_DIM:])
    kv_mine = low(jnp.where(core_id == 0, rotate(kv_raw, cos_table, sin_table), kv_raw))
    kv_other = exchange(kv_mine, "core")
    keys = jnp.where(core_id == 0, kv_mine, kv_other)
    values = jnp.where(core_id == 0, kv_other, kv_mine)
    tanh_part = jnp.tanh(dot_t(queries, keys) * (scale / SOFT_CAP))
    capped = jnp.where(allowed, SOFT_CAP * tanh_part, -1e30)
    top_score = jnp.max(capped, -1, keepdims=True)
    exp_scores = jnp.exp(capped - top_score)
    exp_total = jnp.sum(exp_scores, -1, keepdims=True)
    probs = exp_scores / exp_total
    probs_low = low(probs)
    attended = low(dot(probs_low, values))
    branch = scatter_rows(low(dot_t(attended, head_out)), HEAD_AXES).astype(jnp.float32)
    hidden_in = inputs + rms_norm(branch, gains[1])

    normed_two = gather_rows(low(rms_norm(hidden_in, gains[2])), TENSOR)
    gate_up = dot(normed_two, own_gate_up)
    gate_part, up_part = gate_up[:, :ff_own], gate_up[:, ff_own:]
    activated = low(gated_unit(gate_part, up_part))
    lowered = scatter_rows(low(dot_t(activated, own_down)), TENSOR).astype(jnp.float32)
    output = low(hidden_in + rms_norm(lowered, gains[3]))[None]

    upstream = cotangent[0].astype(jnp.float32)
    grad_lowered, gain_three = norm_back(lowered, gains[3], upstream)
    grad_lowered = gather_rows(low(grad_lowered), TENSOR)
    grad_activated = dot(grad_lowered, own_down)
    _, pull_back = jax.vjp(gated_unit, gate_part, up_part)
    grad_gate_up = low(jnp.concatenate(pull_back(grad_activated), 1))
    grad_normed_two = scatter_rows(low(dot_t(grad_gate_up, own_gate_up)), TENSOR).astype(
        jnp.float32
    )
    term_gate_up = low(t_dot(normed_two, grad_gate_up))
    term_down = low(t_dot(grad_lowered, activated))

    def ff_grad(term):
        return columns_back(
            scatter_rows(term, ("row",) + PLANE), TENSOR, tensor_parts
        ).astype(jnp.float32)

    sum_gate_up = ff_grad(term_gate_up)
    grad_gate_up_w = jnp.concatenate(
        [
            sum_gate_up[:, :, :ff_own].reshape(own_rows, ff_width),
            sum_gate_up[:, :, ff_own:].reshape(own_rows, ff_width),
        ],
        1,
    )
    grad_down = ff_grad(term_down).reshape(own_rows, ff_width)

    grad_hidden_part, gain_two = norm_back(hidden_in, gains[2], grad_normed_two)
    grad_hidden = upstream + grad_hidden_part
    grad_branch, gain_one = norm_back(branch, gains[1], grad_hidden)
    grad_branch = gather_rows(low(grad_branch), HEAD_AXES)

    grad_attended = low(dot(grad_branch, head_out))
    grad_probs = dot_t(grad_attended, values)
    inner_sum = jnp.sum(probs * grad_probs, -1, keepdims=True)
    grad_raw = low(probs * (grad_probs - inner_sum) * (1.0 - tanh_part * tanh_part))
    grad_queries = dot(grad_raw, keys) * scale
    key_terms = t_dot(grad_raw, queries) * scale
    value_terms = t_dot(probs_low, grad_attended)
    kv_terms = jnp.where(core_id == 0, key_terms, value_terms) + exchange(
        jnp.where(core_id == 0, value_terms, key_terms), "core"
    )
    if row_parts > 1:
        kv_terms = scatter_rows(kv_terms, "row")
    kv_back = jnp.where(core_id == 0, rotate(kv_terms, query_cos, -query_sin), kv_terms)
    grad_projected = low(
        jnp.concatenate([rotate(grad_queries, query_cos, -query_sin), kv_back], 1)
    )
    grad_normed_one = scatter_rows(low(dot_t(grad_projected, head_qkv)), HEAD_AXES).astype(
        jnp.float32
    )
    grad_input_part, gain_zero = norm_back(inputs, gains[0], grad_normed_one)
    token_grad = low(grad_hidden + grad_input_part)[None]

    def head_grad(term):
        term = low(term)
        if row_parts > 1:
            term = scatter_rows(term, "row")
        by_owner = jnp.transpose(
            term.reshape(HEADS, fsdp_count, own_rows, -1), (1, 0, 2, 3)
        ).reshape(term.shape)
        return columns_back(scatter_rows(by_owner, "fsdp"), HEAD_AXES, HEADS).astype(jnp.float32)

    grad_out = head_grad(t_dot(grad_branch, attended)).reshape(own_rows, q_width)
    sum_qkv = head_grad(t_dot(normed_query, grad_projected))
    kv_sum = sum_qkv[:, :, HEAD_DIM:].reshape(own_rows, KV_HEADS, 2, HEAD_DIM)
    grad_qkv = jnp.concatenate(
        [
            sum_qkv[:, :, :HEAD_DIM].reshape(own_rows, q_width),
            kv_sum[:, :, 0].reshape(own_rows, kv_width),
            kv_sum[:, :, 1].reshape(own_rows, kv_width),
        ],
        1,
    )
    gain_terms = jnp.stack([gain_zero, gain_one, gain_two, gain_three], 0)
    grad_gains = jnp.sum(
        lax.all_to_all(
            gain_terms.reshape(4, -1, own_rows), EVERY, split_axis=1, concat_axis=1, tiled=True
        ),
        1,
    )
    moment_qkv, square_qkv, new_qkv = adamw(
        w_qkv, first_qkv, second_qkv, grad_qkv, MATRIX_RATE, WEIGHT_DECAY
    )
    moment_out, square_out, new_out = adamw(
        w_out, first_out, second_out, grad_out, MATRIX_RATE, WEIGHT_DECAY
    )
    moment_gate_up, square_gate_up, new_gate_up = adamw(
        w_gate_up, first_gate_up, second_gate_up, grad_gate_up_w, MATRIX_RATE, WEIGHT_DECAY
    )
    moment_down, square_down, new_down = adamw(
        w_down, first_down, second_down, grad_down, MATRIX_RATE, WEIGHT_DECAY
    )
    moment_gains, square_gains, new_gains = adamw(
        norm_gains, first_gains, second_gains, grad_gains, GAIN_RATE, 0.0
    )
    return (
        output,
        token_grad,
        moment_qkv,
        moment_out,
        moment_gate_up,
        moment_down,
        moment_gains,
        square_qkv,
        square_out,
        square_gate_up,
        square_down,
        square_gains,
        new_qkv,
        new_out,
        new_gate_up,
        new_down,
        new_gains,
    )


def solution(mesh):
    ctx_count, fsdp_count = mesh.shape["ctx"], mesh.shape["fsdp"]
    fine_mesh = Mesh(mesh.devices.reshape(ctx_count // HEADS, 2, 2, 2, fsdp_count), EVERY)
    rows = P("fsdp", CTX, None)
    weight = P(EVERY, None)
    gain = P(None, EVERY)
    weights = (weight, weight, weight, weight, gain)
    return jax.shard_map(
        per_device,
        mesh=fine_mesh,
        in_specs=(rows, rows, P()) + weights * 3,
        out_specs=(rows, rows) + weights * 3,
        check_vma=False,
    )
```

```python
import jax
import jax.numpy as jnp
from jax import lax
from jax.sharding import Mesh
from jax.sharding import PartitionSpec as P

HEADS = 8
KV_HEADS = 4
HEAD_DIM = 256
STEP = 5


SOFT_CAP = 3.0
NORM_EPS = 1e-06
BETA_ONE = 0.9
BETA_TWO = 0.95
ADAM_EPS = 1e-08
MATRIX_RATE = 0.02
GAIN_RATE = 0.3
WEIGHT_DECAY = 0.1

PLANE = ("y", "x")
HEAD_AXES = ("y", "x", "core")
CTX = ("row", "y", "x", "core")
TENSOR = ("core", "fsdp")
EVERY = ("row", "y", "x", "core", "fsdp")


def rms_norm(values, gain_row):
    return values * lax.rsqrt(jnp.mean(values * values, -1, keepdims=True) + NORM_EPS) * gain_row


def norm_back(values, gain_row, grad_out):
    _, pull_back = jax.vjp(rms_norm, values, gain_row)
    grad_values, grad_gain = pull_back(grad_out)
    return (grad_values, jnp.sum(grad_gain.reshape(-1, grad_gain.shape[-1]), 0))


def gelu_tanh(values):
    return (
        0.5
        * values
        * (1.0 + jnp.tanh(0.7978845608028654 * (values + 0.044715 * values * values * values)))
    )


def gated_unit(gate_part, up_part):
    return gelu_tanh(gate_part) * up_part


def rotate(values, cos_table, sin_table):
    half_dim = values.shape[-1] // 2
    front_half = values[..., :half_dim]
    back_half = values[..., half_dim:]
    return jnp.concatenate(
        [
            front_half * cos_table - back_half * sin_table,
            back_half * cos_table + front_half * sin_table,
        ],
        -1,
    )


def rope_tables(positions, head_size):
    frequency = 10000.0 ** (-(jnp.arange(head_size // 2, dtype=jnp.float32) * 2.0) / head_size)
    turned = positions.astype(jnp.float32)[:, None] * frequency[None, :]
    return (jnp.cos(turned), jnp.sin(turned))


def positions_of(slot_table, row_total, block_size):
    row_ids = jnp.arange(row_total, dtype=jnp.int32)
    slot_ids = row_ids // block_size
    picked = jnp.sum(
        jnp.where(
            slot_ids[:, None] == jnp.arange(slot_table.shape[0], dtype=jnp.int32)[None, :],
            slot_table[None, :],
            0,
        ),
        1,
    )
    return picked * block_size + row_ids % block_size


def adamw(weight, moment_one, moment_two, gradient, rate, decay):
    first_new = BETA_ONE * moment_one + (1.0 - BETA_ONE) * gradient
    second_new = BETA_TWO * moment_two + (1.0 - BETA_TWO) * gradient * gradient
    step_size = (
        first_new
        / (1.0 - BETA_ONE**STEP)
        / (jnp.sqrt(second_new / (1.0 - BETA_TWO**STEP)) + ADAM_EPS)
    )
    return (first_new, second_new, weight - rate * (step_size + decay * weight))


def low(values):
    return values.astype(jnp.bfloat16)


def dot(left, right):
    return jnp.dot(left, right, preferred_element_type=jnp.float32)


def dot_t(left, right):
    return lax.dot_general(left, right, (((1,), (1,)), ((), ())), preferred_element_type=jnp.float32)


def t_dot(left, right):
    return lax.dot_general(left, right, (((0,), (0,)), ((), ())), preferred_element_type=jnp.float32)


def gather_rows(piece, axes):
    return lax.all_gather(piece, axes, axis=0, tiled=True)


def scatter_rows(terms, axes):
    return lax.psum_scatter(terms, axes, scatter_dimension=0, tiled=True)


def exchange(piece, axis):
    return lax.ppermute(piece, axis, [(0, 1), (1, 0)])


def zero_after(*earlier):
    zero = jnp.float32(0)
    for array in earlier:
        first = lax.slice(array, (0,) * array.ndim, (1,) * array.ndim).reshape(())
        zero = zero + jnp.minimum(jnp.abs(first.astype(jnp.float32)), 0.0)
    return zero


def after(array, *earlier):
    return array + zero_after(*earlier).astype(array.dtype)


def in_order(mine, other, index, axis):
    return jnp.where(index == 0, jnp.stack([mine, other], axis), jnp.stack([other, mine], axis))


def gather_plane_near(block):
    half = block.shape[0] // 2
    return exchange(block[:half], "x"), exchange(block[half:], "y")


def gather_plane_far(block, near, zero=0.0):
    x_id, y_id = lax.axis_index("x"), lax.axis_index("y")
    half = block.shape[0] // 2
    upper_row = in_order(block[:half], near[0], x_id, 0)
    lower_column = in_order(block[half:], near[1], y_id, 0)
    upper_all = in_order(upper_row, exchange(upper_row, "y"), y_id, 0)
    lower_all = in_order(lower_column, exchange(lower_column, "x"), x_id, 1)
    whole = jnp.concatenate([upper_all, lower_all], 2) + jnp.asarray(zero, block.dtype)
    return whole.reshape(4 * block.shape[0], block.shape[1])


def gather_heads(block, earlier):
    plane = gather_plane_far(block, gather_plane_near(block), zero_after(earlier))
    both = in_order(
        plane.reshape((HEADS // 2,) + block.shape),
        exchange(plane, "core").reshape((HEADS // 2,) + block.shape),
        lax.axis_index("core"),
        1,
    )
    return both.reshape(HEADS * block.shape[0], block.shape[1])


def scatter_plane_far(terms):
    x_id, y_id = lax.axis_index("x"), lax.axis_index("y")
    rows, columns = terms.shape[0] // 4, terms.shape[1]
    half = rows // 2
    start = (2 * (1 - y_id) + 1 - x_id) * rows
    upper = lax.dynamic_slice(terms, (start, 0), (half, columns))
    lower = lax.dynamic_slice(terms, (start + half, 0), (half, columns))
    return exchange(upper, "x"), exchange(lower, "y")


def scatter_plane_near(terms, far):
    x_id, y_id = lax.axis_index("x"), lax.axis_index("y")
    rows, columns = terms.shape[0] // 4, terms.shape[1]
    half = rows // 2

    def part(y_at, x_at, first):
        start = (2 * y_at + x_at) * rows + first
        return lax.dynamic_slice(terms, (start, 0), (half, columns))

    def add(left, right):
        return low(left.astype(jnp.float32) + right.astype(jnp.float32))

    upper_far, lower_far = far
    to_y = jnp.concatenate([add(part(1 - y_id, x_id, 0), upper_far), part(1 - y_id, x_id, half)], 0)
    to_x = jnp.concatenate([part(y_id, 1 - x_id, 0), add(part(y_id, 1 - x_id, half), lower_far)], 0)
    return to_y, to_x


def scatter_plane_sum(terms, from_y, from_x):
    x_id, y_id = lax.axis_index("x"), lax.axis_index("y")
    rows, columns = terms.shape[0] // 4, terms.shape[1]
    mine = lax.dynamic_slice(terms, ((2 * y_id + x_id) * rows, 0), (rows, columns))
    return mine.astype(jnp.float32) + from_y.astype(jnp.float32) + from_x.astype(jnp.float32)


def scatter_plane(terms):
    to_y, to_x = scatter_plane_near(terms, scatter_plane_far(terms))
    return scatter_plane_sum(terms, exchange(to_y, "y"), exchange(to_x, "x"))


def my_half(first, second):
    return jnp.where(lax.axis_index("core") == 0, first, second)


def sum_cores(product, array):
    half = array.shape[0] // 2
    first, second = array[:half], array[half:]
    came = exchange(low(product(my_half(second, first))), "core")
    mine = lax.optimization_barrier(low(product(my_half(first, second))))
    return low(mine.astype(jnp.float32) + came.astype(jnp.float32))


def head_terms(terms):
    rows, width = terms.shape
    blocks = terms.reshape(HEADS // 2, 2, rows // HEADS, width)
    came = exchange(my_half(blocks[:, 1], blocks[:, 0]), "core")
    mine = my_half(blocks[:, 0], blocks[:, 1])
    return low(mine.astype(jnp.float32) + came.astype(jnp.float32)).reshape(rows // 2, width)


def over_fsdp(terms, fsdp_count):
    blocks = terms.reshape(fsdp_count, terms.shape[0] // fsdp_count, terms.shape[1])
    return lax.all_to_all(blocks, "fsdp", split_axis=0, concat_axis=0, tiled=True)


def columns_out(weight_piece, axes, parts):
    rows = weight_piece.shape[0]
    blocks = jnp.transpose(weight_piece.reshape(rows, parts, -1), (1, 0, 2))
    return lax.all_to_all(blocks, axes, split_axis=0, concat_axis=0, tiled=True).reshape(
        parts * rows, -1
    )


def blocks_back(grad_piece, axes, parts):
    blocks = grad_piece.reshape(parts, -1, grad_piece.shape[1])
    return lax.all_to_all(blocks, axes, split_axis=0, concat_axis=0, tiled=True)


def side_by_side(blocks):
    parts, rows, columns = blocks.shape
    return jnp.swapaxes(blocks, 0, 1).reshape(rows, parts * columns).astype(jnp.float32)


def per_device(
    tokens,
    cotangent,
    block_order,
    w_qkv,
    w_out,
    w_gate_up,
    w_down,
    norm_gains,
    first_qkv,
    first_out,
    first_gate_up,
    first_down,
    first_gains,
    second_qkv,
    second_out,
    second_gate_up,
    second_down,
    second_gains,
):
    row_count = tokens.shape[1]
    block_size = row_count // 2
    row_parts = lax.axis_size("row")
    fsdp_count = lax.axis_size("fsdp")
    core_id = lax.axis_index("core")
    row_id = lax.axis_index("row")
    seq_length = row_count * row_parts * HEADS
    query_rows = row_count * HEADS
    own_rows = w_qkv.shape[0]
    width = tokens.shape[2]
    q_width = HEADS * HEAD_DIM
    kv_width = KV_HEADS * HEAD_DIM
    ff_width = w_down.shape[1]
    tensor_parts = 2 * fsdp_count
    ff_own = ff_width // tensor_parts
    scale = HEAD_DIM ** (-0.5)

    gate_up_mine = columns_out(
        jnp.concatenate(
            [
                low(w_gate_up[:, :ff_width]).reshape(own_rows, tensor_parts, ff_own),
                low(w_gate_up[:, ff_width:]).reshape(own_rows, tensor_parts, ff_own),
            ],
            2,
        ),
        TENSOR,
        tensor_parts,
    )
    own_gate_up = gather_rows(gate_up_mine, ("row",) + PLANE)
    seq_tokens = gather_rows(tokens[0], CTX)

    def to_heads(pieces):
        copies = jnp.broadcast_to(
            pieces[None, :, None], (row_parts, HEADS, fsdp_count) + pieces.shape[1:]
        ).reshape((-1,) + pieces.shape[1:])
        return lax.all_to_all(copies, EVERY, split_axis=0, concat_axis=0, tiled=True)

    q_cols = low(w_qkv[:, :q_width]).reshape(own_rows, HEADS, HEAD_DIM)
    k_cols = low(w_qkv[:, q_width : q_width + kv_width]).reshape(own_rows, KV_HEADS, 1, HEAD_DIM)
    v_cols = low(w_qkv[:, q_width + kv_width :]).reshape(own_rows, KV_HEADS, 1, HEAD_DIM)
    kv_cols = jnp.concatenate([k_cols, v_cols], 2).reshape(own_rows, HEADS, HEAD_DIM)
    qkv_cols = jnp.concatenate([q_cols, kv_cols], 2)
    gain_piece = jnp.pad(
        low(norm_gains).reshape(1, 1, 4 * own_rows),
        ((0, HEADS - 1), (0, 7), (0, 2 * HEAD_DIM - 4 * own_rows)),
        mode="edge",
    )
    pieces = jnp.concatenate([jnp.swapaxes(qkv_cols, 0, 1), gain_piece], 1)
    received = to_heads(after(pieces, gate_up_mine))
    head_qkv = received[:, :own_rows].reshape(width, 2 * HEAD_DIM)
    gains = (
        jnp.swapaxes(received[:, own_rows, : 4 * own_rows].reshape(-1, 4, own_rows), 0, 1)
        .reshape(4, width)
        .astype(jnp.float32)
    )
    out_pieces = jnp.swapaxes(low(w_out).reshape(own_rows, HEADS, HEAD_DIM), 0, 1)
    head_out = to_heads(after(out_pieces, received)).reshape(width, HEAD_DIM)

    down_mine = columns_out(after(low(w_down), head_out), TENSOR, tensor_parts)

    key_positions = positions_of(block_order, seq_length, block_size)
    cos_table, sin_table = rope_tables(key_positions, HEAD_DIM)
    first_row = row_id * query_rows

    def query_part(array):
        if row_parts == 1:
            return array
        return lax.dynamic_slice_in_dim(array, first_row, query_rows, 0)

    query_cos, query_sin = query_part(cos_table), query_part(sin_table)
    allowed = key_positions[None, :] <= query_part(key_positions)[:, None]

    inputs = tokens[0].astype(jnp.float32)
    normed_one = low(rms_norm(seq_tokens.astype(jnp.float32), gains[0]))
    normed_query = query_part(normed_one)
    queries = low(rotate(dot(normed_query, head_qkv[:, :HEAD_DIM]), query_cos, query_sin))
    kv_raw = dot(normed_one, head_qkv[:, HEAD_DIM:])
    kv_mine = low(jnp.where(core_id == 0, rotate(kv_raw, cos_table, sin_table), kv_raw))
    kv_other = exchange(kv_mine, "core")
    keys = jnp.where(core_id == 0, kv_mine, kv_other)
    values = jnp.where(core_id == 0, kv_other, kv_mine)
    tanh_part = jnp.tanh(dot_t(queries, keys) * (scale / SOFT_CAP))
    capped = jnp.where(allowed, SOFT_CAP * tanh_part, -1e30)
    top_score = jnp.max(capped, -1, keepdims=True)
    exp_scores = jnp.exp(capped - top_score)
    exp_total = jnp.sum(exp_scores, -1, keepdims=True)
    probs = exp_scores / exp_total
    probs_low = low(probs)
    attended = low(dot(probs_low, values) + zero_after(head_out))
    branch = scatter_plane(head_terms(low(dot_t(attended, head_out))))
    hidden_in = inputs + rms_norm(branch, gains[1])

    normed_two_mine = low(rms_norm(hidden_in, gains[2]) + zero_after(own_gate_up, down_mine))
    normed_two = gather_rows(normed_two_mine, TENSOR)
    down_mine = after(down_mine, normed_two_mine)
    down_near = gather_plane_near(down_mine)
    gate_up = dot(normed_two, own_gate_up)
    gate_part, up_part = gate_up[:, :ff_own], gate_up[:, ff_own:]
    own_down = gather_plane_far(down_mine, down_near, zero_after(gate_up))
    if row_parts > 1:
        own_down = gather_rows(own_down, "row")
    activated = low(gated_unit(gate_part, up_part))
    lowered_terms = sum_cores(lambda rows: dot_t(rows, own_down), activated)
    lowered_pieces = over_fsdp(lowered_terms, fsdp_count)
    later_gate_up = after(gate_up, lowered_terms)
    _, pull_back = jax.vjp(gated_unit, later_gate_up[:, :ff_own], later_gate_up[:, ff_own:])
    gate_factor, up_factor = lax.optimization_barrier(pull_back(jnp.ones_like(gate_part)))
    lowered_pieces = after(lowered_pieces, gate_factor, up_factor)
    lowered = jnp.sum(lowered_pieces.astype(jnp.float32), 0)
    output = low(hidden_in + rms_norm(lowered, gains[3]))[None]

    upstream = cotangent[0].astype(jnp.float32)
    grad_lowered, gain_three = norm_back(lowered, gains[3], upstream)
    grad_lowered = gather_rows(low(grad_lowered), TENSOR)
    plane_down = scatter_rows(low(t_dot(grad_lowered, activated)), ("row",) + PLANE)
    grad_activated = dot(grad_lowered, own_down)
    grad_gate_up = low(
        jnp.concatenate([grad_activated * gate_factor, grad_activated * up_factor], 1)
    )
    normed_two_terms = sum_cores(lambda rows: dot_t(rows, own_gate_up), grad_gate_up)
    normed_two_pieces = over_fsdp(normed_two_terms, fsdp_count)
    term_gate = low(t_dot(normed_two, grad_gate_up[:, :ff_own]))
    plane_gate = scatter_rows(term_gate, ("row",) + PLANE)
    normed_two_pieces = after(normed_two_pieces, term_gate)
    grad_normed_two = jnp.sum(normed_two_pieces.astype(jnp.float32), 0)

    grad_hidden_part, gain_two = norm_back(hidden_in, gains[2], grad_normed_two)
    grad_hidden = upstream + grad_hidden_part
    grad_branch, gain_one = norm_back(branch, gains[1], grad_hidden)
    grad_branch_mine = low(grad_branch)
    later_rows = after(normed_two, grad_branch_mine)
    plane_up = scatter_rows(
        low(t_dot(later_rows, grad_gate_up[:, ff_own:])), ("row",) + PLANE
    )
    blocks_down = blocks_back(after(plane_down, normed_two_pieces), TENSOR, tensor_parts)
    grad_branch = gather_heads(grad_branch_mine, blocks_down)
    blocks_gate = blocks_back(after(plane_gate, blocks_down), TENSOR, tensor_parts)
    blocks_up = blocks_back(after(plane_up, blocks_gate), TENSOR, tensor_parts)

    grad_attended = low(dot(grad_branch, head_out))
    grad_probs = dot_t(grad_attended, values)
    inner_sum = jnp.sum(probs * grad_probs, -1, keepdims=True)
    grad_raw = low(probs * (grad_probs - inner_sum) * (1.0 - tanh_part * tanh_part))
    grad_queries = dot(grad_raw, keys) * scale
    key_terms = t_dot(grad_raw, queries) * scale
    value_terms = t_dot(probs_low, grad_attended)
    kv_terms = jnp.where(core_id == 0, key_terms, value_terms) + exchange(
        jnp.where(core_id == 0, value_terms, key_terms), "core"
    )
    if row_parts > 1:
        kv_terms = scatter_rows(kv_terms, "row")
    kv_back = jnp.where(core_id == 0, rotate(kv_terms, query_cos, -query_sin), kv_terms)
    grad_projected = low(
        jnp.concatenate([rotate(grad_queries, query_cos, -query_sin), kv_back], 1)
        + zero_after(blocks_gate)
    )
    grad_normed_one = scatter_plane(head_terms(low(dot_t(grad_projected, head_qkv))))
    grad_input_part, gain_zero = norm_back(inputs, gains[0], grad_normed_one)
    token_grad = low(grad_hidden + grad_input_part)[None]

    def to_owners(term):
        blocks = term.reshape(row_parts * HEADS * fsdp_count, -1, term.shape[1])
        return lax.all_to_all(blocks, EVERY, split_axis=0, concat_axis=0, tiled=True)

    def head_grad(pieces):
        pieces = pieces.reshape((row_parts, HEADS, fsdp_count) + pieces.shape[1:])
        return jnp.swapaxes(jnp.sum(pieces.astype(jnp.float32), (0, 2)), 0, 1)

    qkv_pieces = to_owners(after(low(t_dot(normed_query, grad_projected)), blocks_up))
    sum_qkv = head_grad(qkv_pieces)

    gain_terms = jnp.stack([gain_zero, gain_one, gain_two, gain_three], 0)
    gain_terms = jnp.swapaxes(gain_terms.reshape(4, -1, own_rows), 0, 1).reshape(-1, 4 * own_rows)
    gain_high = low(gain_terms)
    gain_low = low(gain_terms - gain_high.astype(jnp.float32))
    gain_rows = jnp.pad(
        jnp.concatenate([gain_high, gain_low], 1), ((0, 0), (0, 8 * HEAD_DIM - 8 * own_rows))
    ).reshape(-1, 8, HEAD_DIM)
    out_term = after(low(t_dot(grad_branch, attended)), qkv_pieces)
    out_pieces = to_owners(
        jnp.concatenate([out_term.reshape(-1, own_rows, HEAD_DIM), gain_rows], 1).reshape(
            -1, HEAD_DIM
        )
    )
    grad_out = head_grad(out_pieces[:, :own_rows]).reshape(own_rows, q_width)
    grad_gains = jnp.sum(
        out_pieces[:, own_rows:].reshape(-1, 8 * HEAD_DIM)[:, : 8 * own_rows].astype(jnp.float32),
        0,
    ).reshape(2, 4, own_rows).sum(0)
    kv_sum = sum_qkv[:, :, HEAD_DIM:].reshape(own_rows, KV_HEADS, 2, HEAD_DIM)
    grad_qkv = jnp.concatenate(
        [
            sum_qkv[:, :, :HEAD_DIM].reshape(own_rows, q_width),
            kv_sum[:, :, 0].reshape(own_rows, kv_width),
            kv_sum[:, :, 1].reshape(own_rows, kv_width),
        ],
        1,
    )
    grad_down = side_by_side(blocks_down)
    grad_gate_up_w = jnp.concatenate([side_by_side(blocks_gate), side_by_side(blocks_up)], 1)
    moment_qkv, square_qkv, new_qkv = adamw(
        w_qkv, first_qkv, second_qkv, grad_qkv, MATRIX_RATE, WEIGHT_DECAY
    )
    moment_out, square_out, new_out = adamw(
        w_out, first_out, second_out, grad_out, MATRIX_RATE, WEIGHT_DECAY
    )
    moment_gate_up, square_gate_up, new_gate_up = adamw(
        w_gate_up, first_gate_up, second_gate_up, grad_gate_up_w, MATRIX_RATE, WEIGHT_DECAY
    )
    moment_down, square_down, new_down = adamw(
        w_down, first_down, second_down, grad_down, MATRIX_RATE, WEIGHT_DECAY
    )
    moment_gains, square_gains, new_gains = adamw(
        norm_gains, first_gains, second_gains, grad_gains, GAIN_RATE, 0.0
    )
    return (
        output,
        token_grad,
        moment_qkv,
        moment_out,
        moment_gate_up,
        moment_down,
        moment_gains,
        square_qkv,
        square_out,
        square_gate_up,
        square_down,
        square_gains,
        new_qkv,
        new_out,
        new_gate_up,
        new_down,
        new_gains,
    )


def solution(mesh):
    ctx_count, fsdp_count = mesh.shape["ctx"], mesh.shape["fsdp"]
    fine_mesh = Mesh(mesh.devices.reshape(ctx_count // HEADS, 2, 2, 2, fsdp_count), EVERY)
    rows = P("fsdp", CTX, None)
    weight = P(EVERY, None)
    gain = P(None, EVERY)
    weights = (weight, weight, weight, weight, gain)
    return jax.shard_map(
        per_device,
        mesh=fine_mesh,
        in_specs=(rows, rows, P()) + weights * 3,
        out_specs=(rows, rows) + weights * 3,
        check_vma=False,
    )
```

```python
import jax
import jax.numpy as jnp
from jax import lax
from jax.sharding import Mesh
from jax.sharding import PartitionSpec as P

HEADS = 8
KV_HEADS = 4
HEAD_DIM = 256
STEP = 5


SOFT_CAP = 3.0
NORM_EPS = 1e-06
BETA_ONE = 0.9
BETA_TWO = 0.95
ADAM_EPS = 1e-08
MATRIX_RATE = 0.02
GAIN_RATE = 0.3
WEIGHT_DECAY = 0.1

PLANE = ("y", "x")
HEAD_AXES = ("y", "x", "core")
CTX = ("row", "y", "x", "core")
TENSOR = ("core", "fsdp")
EVERY = ("row", "y", "x", "core", "fsdp")


def rms_norm(values, gain_row):
    return values * lax.rsqrt(jnp.mean(values * values, -1, keepdims=True) + NORM_EPS) * gain_row


def norm_back(values, gain_row, grad_out):
    _, pull_back = jax.vjp(rms_norm, values, gain_row)
    grad_values, grad_gain = pull_back(grad_out)
    return (grad_values, jnp.sum(grad_gain.reshape(-1, grad_gain.shape[-1]), 0))


def gelu_tanh(values):
    return (
        0.5
        * values
        * (1.0 + jnp.tanh(0.7978845608028654 * (values + 0.044715 * values * values * values)))
    )


def gated_unit(gate_part, up_part):
    return gelu_tanh(gate_part) * up_part


def rotate(values, cos_table, sin_table):
    half_dim = values.shape[-1] // 2
    front_half = values[..., :half_dim]
    back_half = values[..., half_dim:]
    return jnp.concatenate(
        [
            front_half * cos_table - back_half * sin_table,
            back_half * cos_table + front_half * sin_table,
        ],
        -1,
    )


def rope_tables(positions, head_size):
    frequency = 10000.0 ** (-(jnp.arange(head_size // 2, dtype=jnp.float32) * 2.0) / head_size)
    turned = positions.astype(jnp.float32)[:, None] * frequency[None, :]
    return (jnp.cos(turned), jnp.sin(turned))


def positions_of(slot_table, row_total, block_size):
    row_ids = jnp.arange(row_total, dtype=jnp.int32)
    slot_ids = row_ids // block_size
    picked = jnp.sum(
        jnp.where(
            slot_ids[:, None] == jnp.arange(slot_table.shape[0], dtype=jnp.int32)[None, :],
            slot_table[None, :],
            0,
        ),
        1,
    )
    return picked * block_size + row_ids % block_size


def adamw(weight, moment_one, moment_two, gradient, rate, decay):
    first_new = BETA_ONE * moment_one + (1.0 - BETA_ONE) * gradient
    second_new = BETA_TWO * moment_two + (1.0 - BETA_TWO) * gradient * gradient
    step_size = (
        first_new
        / (1.0 - BETA_ONE**STEP)
        / (jnp.sqrt(second_new / (1.0 - BETA_TWO**STEP)) + ADAM_EPS)
    )
    return (first_new, second_new, weight - rate * (step_size + decay * weight))


def low(values):
    return values.astype(jnp.bfloat16)


def dot(left, right):
    return jnp.dot(left, right, preferred_element_type=jnp.float32)


def dot_t(left, right):
    return lax.dot_general(left, right, (((1,), (1,)), ((), ())), preferred_element_type=jnp.float32)


def t_dot(left, right):
    return lax.dot_general(left, right, (((0,), (0,)), ((), ())), preferred_element_type=jnp.float32)


def gather_rows(piece, axes):
    return lax.all_gather(piece, axes, axis=0, tiled=True)


def scatter_rows(terms, axes):
    return lax.psum_scatter(terms, axes, scatter_dimension=0, tiled=True)


def exchange(piece, axis):
    return lax.ppermute(piece, axis, [(0, 1), (1, 0)])


def zero_after(*earlier):
    zero = jnp.float32(0)
    for array in earlier:
        first = lax.slice(array, (0,) * array.ndim, (1,) * array.ndim).reshape(())
        zero = zero + jnp.minimum(jnp.abs(first.astype(jnp.float32)), 0.0)
    return zero


def after(array, *earlier):
    return array + zero_after(*earlier).astype(array.dtype)


def in_order(mine, other, index, axis):
    return jnp.where(index == 0, jnp.stack([mine, other], axis), jnp.stack([other, mine], axis))


def gather_plane_near(block):
    half = block.shape[0] // 2
    return exchange(block[:half], "x"), exchange(block[half:], "y")


def gather_plane_far(block, near, zero=0.0):
    x_id, y_id = lax.axis_index("x"), lax.axis_index("y")
    half = block.shape[0] // 2
    upper_row = in_order(block[:half], near[0], x_id, 0)
    lower_column = in_order(block[half:], near[1], y_id, 0)
    upper_all = in_order(upper_row, exchange(upper_row, "y"), y_id, 0)
    lower_all = in_order(lower_column, exchange(lower_column, "x"), x_id, 1)
    whole = jnp.concatenate([upper_all, lower_all], 2) + jnp.asarray(zero, block.dtype)
    return whole.reshape(4 * block.shape[0], block.shape[1])


def gather_heads(block, earlier):
    plane = gather_plane_far(block, gather_plane_near(block), zero_after(earlier))
    both = in_order(
        plane.reshape((HEADS // 2,) + block.shape),
        exchange(plane, "core").reshape((HEADS // 2,) + block.shape),
        lax.axis_index("core"),
        1,
    )
    return both.reshape(HEADS * block.shape[0], block.shape[1])


def scatter_plane_far(terms):
    x_id, y_id = lax.axis_index("x"), lax.axis_index("y")
    rows, columns = terms.shape[0] // 4, terms.shape[1]
    half = rows // 2
    start = (2 * (1 - y_id) + 1 - x_id) * rows
    upper = lax.dynamic_slice(terms, (start, 0), (half, columns))
    lower = lax.dynamic_slice(terms, (start + half, 0), (half, columns))
    return exchange(upper, "x"), exchange(lower, "y")


def scatter_plane_near(terms, far):
    x_id, y_id = lax.axis_index("x"), lax.axis_index("y")
    rows, columns = terms.shape[0] // 4, terms.shape[1]
    half = rows // 2

    def part(y_at, x_at, first):
        start = (2 * y_at + x_at) * rows + first
        return lax.dynamic_slice(terms, (start, 0), (half, columns))

    def add(left, right):
        return low(left.astype(jnp.float32) + right.astype(jnp.float32))

    upper_far, lower_far = far
    to_y = jnp.concatenate([add(part(1 - y_id, x_id, 0), upper_far), part(1 - y_id, x_id, half)], 0)
    to_x = jnp.concatenate([part(y_id, 1 - x_id, 0), add(part(y_id, 1 - x_id, half), lower_far)], 0)
    return to_y, to_x


def scatter_plane_sum(terms, from_y, from_x):
    x_id, y_id = lax.axis_index("x"), lax.axis_index("y")
    rows, columns = terms.shape[0] // 4, terms.shape[1]
    mine = lax.dynamic_slice(terms, ((2 * y_id + x_id) * rows, 0), (rows, columns))
    return mine.astype(jnp.float32) + from_y.astype(jnp.float32) + from_x.astype(jnp.float32)


def scatter_plane(terms):
    to_y, to_x = scatter_plane_near(terms, scatter_plane_far(terms))
    return scatter_plane_sum(terms, exchange(to_y, "y"), exchange(to_x, "x"))


def my_half(first, second):
    return jnp.where(lax.axis_index("core") == 0, first, second)


def sum_cores(product, array):
    half = array.shape[0] // 2
    first, second = array[:half], array[half:]
    came = exchange(low(product(my_half(second, first))), "core")
    mine = lax.optimization_barrier(low(product(my_half(first, second))))
    return low(mine.astype(jnp.float32) + came.astype(jnp.float32))


def head_terms(terms):
    rows, width = terms.shape
    blocks = terms.reshape(HEADS // 2, 2, rows // HEADS, width)
    came = exchange(my_half(blocks[:, 1], blocks[:, 0]), "core")
    mine = my_half(blocks[:, 0], blocks[:, 1])
    return low(mine.astype(jnp.float32) + came.astype(jnp.float32)).reshape(rows // 2, width)


def over_fsdp(terms, fsdp_count):
    blocks = terms.reshape(fsdp_count, terms.shape[0] // fsdp_count, terms.shape[1])
    return lax.all_to_all(blocks, "fsdp", split_axis=0, concat_axis=0, tiled=True)


def columns_out(weight_piece, axes, parts):
    rows = weight_piece.shape[0]
    blocks = jnp.transpose(weight_piece.reshape(rows, parts, -1), (1, 0, 2))
    return lax.all_to_all(blocks, axes, split_axis=0, concat_axis=0, tiled=True).reshape(
        parts * rows, -1
    )


def blocks_back(grad_piece, axes, parts):
    blocks = grad_piece.reshape(parts, -1, grad_piece.shape[1])
    return lax.all_to_all(blocks, axes, split_axis=0, concat_axis=0, tiled=True)


def side_by_side(blocks):
    parts, rows, columns = blocks.shape
    return jnp.swapaxes(blocks, 0, 1).reshape(rows, parts * columns).astype(jnp.float32)


def per_device(
    tokens,
    cotangent,
    block_order,
    w_qkv,
    w_out,
    w_gate_up,
    w_down,
    norm_gains,
    first_qkv,
    first_out,
    first_gate_up,
    first_down,
    first_gains,
    second_qkv,
    second_out,
    second_gate_up,
    second_down,
    second_gains,
):
    row_count = tokens.shape[1]
    block_size = row_count // 2
    row_parts = lax.axis_size("row")
    fsdp_count = lax.axis_size("fsdp")
    core_id = lax.axis_index("core")
    row_id = lax.axis_index("row")
    seq_length = row_count * row_parts * HEADS
    query_rows = row_count * HEADS
    own_rows = w_qkv.shape[0]
    width = tokens.shape[2]
    q_width = HEADS * HEAD_DIM
    kv_width = KV_HEADS * HEAD_DIM
    ff_width = w_down.shape[1]
    tensor_parts = 2 * fsdp_count
    ff_own = ff_width // tensor_parts
    scale = HEAD_DIM ** (-0.5)

    gate_up_mine = columns_out(
        jnp.concatenate(
            [
                low(w_gate_up[:, :ff_width]).reshape(own_rows, tensor_parts, ff_own),
                low(w_gate_up[:, ff_width:]).reshape(own_rows, tensor_parts, ff_own),
            ],
            2,
        ),
        TENSOR,
        tensor_parts,
    )
    own_gate_up = gather_rows(gate_up_mine, ("row",) + PLANE)
    seq_tokens = gather_rows(tokens[0], CTX)

    def to_heads(pieces):
        copies = jnp.broadcast_to(
            pieces[None, :, None], (row_parts, HEADS, fsdp_count) + pieces.shape[1:]
        ).reshape((-1,) + pieces.shape[1:])
        return lax.all_to_all(copies, EVERY, split_axis=0, concat_axis=0, tiled=True)

    q_cols = low(w_qkv[:, :q_width]).reshape(own_rows, HEADS, HEAD_DIM)
    k_cols = low(w_qkv[:, q_width : q_width + kv_width]).reshape(own_rows, KV_HEADS, 1, HEAD_DIM)
    v_cols = low(w_qkv[:, q_width + kv_width :]).reshape(own_rows, KV_HEADS, 1, HEAD_DIM)
    kv_cols = jnp.concatenate([k_cols, v_cols], 2).reshape(own_rows, HEADS, HEAD_DIM)
    qkv_cols = jnp.concatenate([q_cols, kv_cols], 2)
    gain_piece = jnp.pad(
        low(norm_gains).reshape(1, 1, 4 * own_rows),
        ((0, HEADS - 1), (0, 7), (0, 2 * HEAD_DIM - 4 * own_rows)),
        mode="edge",
    )
    pieces = jnp.concatenate([jnp.swapaxes(qkv_cols, 0, 1), gain_piece], 1)
    received = to_heads(after(pieces, gate_up_mine))
    head_qkv = received[:, :own_rows].reshape(width, 2 * HEAD_DIM)
    gains = (
        jnp.swapaxes(received[:, own_rows, : 4 * own_rows].reshape(-1, 4, own_rows), 0, 1)
        .reshape(4, width)
        .astype(jnp.float32)
    )
    out_pieces = jnp.swapaxes(low(w_out).reshape(own_rows, HEADS, HEAD_DIM), 0, 1)
    head_out = to_heads(after(out_pieces, received)).reshape(width, HEAD_DIM)

    down_mine = columns_out(after(low(w_down), head_out), TENSOR, tensor_parts)

    key_positions = positions_of(block_order, seq_length, block_size)
    cos_table, sin_table = rope_tables(key_positions, HEAD_DIM)
    first_row = row_id * query_rows

    def query_part(array):
        if row_parts == 1:
            return array
        return lax.dynamic_slice_in_dim(array, first_row, query_rows, 0)

    query_cos, query_sin = query_part(cos_table), query_part(sin_table)
    allowed = key_positions[None, :] <= query_part(key_positions)[:, None]

    inputs = tokens[0].astype(jnp.float32)
    normed_one = low(rms_norm(seq_tokens.astype(jnp.float32), gains[0]))
    normed_query = query_part(normed_one)
    queries = low(rotate(dot(normed_query, head_qkv[:, :HEAD_DIM]), query_cos, query_sin))
    kv_raw = dot(normed_one, head_qkv[:, HEAD_DIM:])
    kv_mine = low(jnp.where(core_id == 0, rotate(kv_raw, cos_table, sin_table), kv_raw))
    kv_other = exchange(kv_mine, "core")
    keys = jnp.where(core_id == 0, kv_mine, kv_other)
    values = jnp.where(core_id == 0, kv_other, kv_mine)
    tanh_part = jnp.tanh(dot_t(queries, keys) * (scale / SOFT_CAP))
    capped = jnp.where(allowed, SOFT_CAP * tanh_part, -1e30)
    top_score = jnp.max(capped, -1, keepdims=True)
    exp_scores = jnp.exp(capped - top_score)
    exp_total = jnp.sum(exp_scores, -1, keepdims=True)
    probs = exp_scores / exp_total
    probs_low = low(probs)
    attended = low(dot(probs_low, values) + zero_after(head_out))
    branch = scatter_plane(head_terms(low(dot_t(attended, head_out))))
    hidden_in = after(inputs, own_gate_up, down_mine) + rms_norm(branch, gains[1])

    normed_two_mine = low(rms_norm(hidden_in, gains[2]))
    normed_two = gather_rows(normed_two_mine, TENSOR)
    down_mine = after(down_mine, normed_two_mine)
    down_near = gather_plane_near(down_mine)
    gate_up = dot(normed_two, own_gate_up)
    gate_part, up_part = gate_up[:, :ff_own], gate_up[:, ff_own:]
    own_down = gather_plane_far(down_mine, down_near, zero_after(gate_up))
    if row_parts > 1:
        own_down = gather_rows(own_down, "row")
    activated = low(gated_unit(gate_part, up_part))
    lowered_terms = sum_cores(lambda rows: dot_t(rows, own_down), activated)
    lowered_pieces = over_fsdp(lowered_terms, fsdp_count)
    later_gate_up = after(gate_up, lowered_terms)
    _, pull_back = jax.vjp(gated_unit, later_gate_up[:, :ff_own], later_gate_up[:, ff_own:])
    gate_factor, up_factor = lax.optimization_barrier(pull_back(jnp.ones_like(gate_part)))
    lowered_pieces = after(lowered_pieces, gate_factor, up_factor)
    lowered = jnp.sum(lowered_pieces.astype(jnp.float32), 0)
    output = low(hidden_in + rms_norm(lowered, gains[3]))[None]

    upstream = cotangent[0].astype(jnp.float32)
    grad_lowered, gain_three = norm_back(lowered, gains[3], upstream)
    grad_lowered = gather_rows(low(grad_lowered), TENSOR)
    plane_down = scatter_rows(low(t_dot(grad_lowered, activated)), ("row",) + PLANE)
    grad_activated = dot(grad_lowered, own_down)
    grad_gate_up = low(
        jnp.concatenate([grad_activated * gate_factor, grad_activated * up_factor], 1)
    )
    normed_two_halves = low(dot_t(grad_gate_up, own_gate_up))
    half = normed_two_halves.shape[0] // 2
    sent = my_half(normed_two_halves[half:], normed_two_halves[:half])
    normed_two_terms = low(
        my_half(normed_two_halves[:half], normed_two_halves[half:]).astype(jnp.float32)
        + exchange(sent, "core").astype(jnp.float32)
    )
    normed_two_pieces = over_fsdp(normed_two_terms, fsdp_count)
    term_gate = low(t_dot(normed_two, after(grad_gate_up[:, :ff_own], normed_two_terms)))
    plane_gate = scatter_rows(term_gate, ("row",) + PLANE)
    term_up = low(t_dot(normed_two, after(grad_gate_up[:, ff_own:], term_gate)))
    plane_up = scatter_rows(term_up, ("row",) + PLANE)
    normed_two_pieces = after(normed_two_pieces, term_up, plane_down)
    grad_normed_two = jnp.sum(normed_two_pieces.astype(jnp.float32), 0)

    grad_hidden_part, gain_two = norm_back(hidden_in, gains[2], grad_normed_two)
    grad_hidden = upstream + grad_hidden_part
    grad_branch, gain_one = norm_back(branch, gains[1], grad_hidden)
    grad_branch_mine = low(grad_branch)
    blocks_down = blocks_back(after(plane_down, grad_normed_two), TENSOR, tensor_parts)
    grad_branch = gather_heads(grad_branch_mine, blocks_down)
    blocks_gate = blocks_back(plane_gate, TENSOR, tensor_parts)

    grad_attended = low(dot(grad_branch, head_out))
    grad_probs = dot_t(grad_attended, values)
    inner_sum = jnp.sum(probs * grad_probs, -1, keepdims=True)
    grad_raw = low(probs * (grad_probs - inner_sum) * (1.0 - tanh_part * tanh_part))
    grad_queries = dot(grad_raw, keys) * scale
    key_terms = t_dot(grad_raw, queries) * scale
    value_terms = t_dot(probs_low, grad_attended)
    kv_terms = jnp.where(core_id == 0, key_terms, value_terms) + exchange(
        jnp.where(core_id == 0, value_terms, key_terms), "core"
    )
    if row_parts > 1:
        kv_terms = scatter_rows(kv_terms, "row")
    kv_back = jnp.where(core_id == 0, rotate(kv_terms, query_cos, -query_sin), kv_terms)
    grad_projected = low(
        jnp.concatenate([rotate(grad_queries, query_cos, -query_sin), kv_back], 1)
        + zero_after(blocks_gate)
    )
    grad_normed_one = scatter_plane(head_terms(low(dot_t(grad_projected, head_qkv))))
    grad_input_part, gain_zero = norm_back(inputs, gains[0], grad_normed_one)
    token_grad = low(grad_hidden + grad_input_part)[None]

    def to_owners(term):
        blocks = term.reshape(row_parts * HEADS * fsdp_count, -1, term.shape[1])
        return lax.all_to_all(blocks, EVERY, split_axis=0, concat_axis=0, tiled=True)

    def head_grad(pieces):
        pieces = pieces.reshape((row_parts, HEADS, fsdp_count) + pieces.shape[1:])
        return jnp.swapaxes(jnp.sum(pieces.astype(jnp.float32), (0, 2)), 0, 1)

    out_term = lax.optimization_barrier(low(t_dot(grad_branch, attended)))
    out_pieces = to_owners(out_term)
    blocks_up = blocks_back(plane_up, TENSOR, tensor_parts)
    qkv_term = low(t_dot(normed_query, grad_projected))
    if row_parts > 1:
        qkv_term = scatter_rows(qkv_term, "row")
    by_owner = jnp.swapaxes(qkv_term.reshape(HEADS, fsdp_count, own_rows, -1), 0, 1)
    qkv_mine = scatter_rows(by_owner.reshape(qkv_term.shape), "fsdp")
    qkv_blocks = blocks_back(qkv_mine, HEAD_AXES, HEADS)
    sum_qkv = jnp.swapaxes(qkv_blocks, 0, 1).astype(jnp.float32)
    grad_out = head_grad(out_pieces).reshape(own_rows, q_width)

    gain_terms = jnp.stack([gain_zero, gain_one, gain_two, gain_three], 0)
    gain_terms = jnp.swapaxes(gain_terms.reshape(4, -1, own_rows), 0, 1)
    gain_pieces = lax.all_to_all(
        after(gain_terms, qkv_blocks), EVERY, split_axis=0, concat_axis=0, tiled=True
    )
    grad_gains = jnp.sum(gain_pieces, 0)
    kv_sum = sum_qkv[:, :, HEAD_DIM:].reshape(own_rows, KV_HEADS, 2, HEAD_DIM)
    grad_qkv = jnp.concatenate(
        [
            sum_qkv[:, :, :HEAD_DIM].reshape(own_rows, q_width),
            kv_sum[:, :, 0].reshape(own_rows, kv_width),
            kv_sum[:, :, 1].reshape(own_rows, kv_width),
        ],
        1,
    )
    grad_down = side_by_side(blocks_down)
    grad_gate_up_w = jnp.concatenate([side_by_side(blocks_gate), side_by_side(blocks_up)], 1)
    moment_qkv, square_qkv, new_qkv = adamw(
        w_qkv, first_qkv, second_qkv, grad_qkv, MATRIX_RATE, WEIGHT_DECAY
    )
    moment_out, square_out, new_out = adamw(
        w_out, first_out, second_out, grad_out, MATRIX_RATE, WEIGHT_DECAY
    )
    moment_gate_up, square_gate_up, new_gate_up = adamw(
        w_gate_up, first_gate_up, second_gate_up, grad_gate_up_w, MATRIX_RATE, WEIGHT_DECAY
    )
    moment_down, square_down, new_down = adamw(
        w_down, first_down, second_down, grad_down, MATRIX_RATE, WEIGHT_DECAY
    )
    moment_gains, square_gains, new_gains = adamw(
        norm_gains, first_gains, second_gains, grad_gains, GAIN_RATE, 0.0
    )
    return (
        output,
        token_grad,
        moment_qkv,
        moment_out,
        moment_gate_up,
        moment_down,
        moment_gains,
        square_qkv,
        square_out,
        square_gate_up,
        square_down,
        square_gains,
        new_qkv,
        new_out,
        new_gate_up,
        new_down,
        new_gains,
    )


def solution(mesh):
    ctx_count, fsdp_count = mesh.shape["ctx"], mesh.shape["fsdp"]
    fine_mesh = Mesh(mesh.devices.reshape(ctx_count // HEADS, 2, 2, 2, fsdp_count), EVERY)
    rows = P("fsdp", CTX, None)
    weight = P(EVERY, None)
    gain = P(None, EVERY)
    weights = (weight, weight, weight, weight, gain)
    return jax.shard_map(
        per_device,
        mesh=fine_mesh,
        in_specs=(rows, rows, P()) + weights * 3,
        out_specs=(rows, rows) + weights * 3,
        check_vma=False,
    )
```

```python
import jax
import jax.numpy as jnp
from jax import lax
from jax.experimental import pallas as pl
from jax.experimental.pallas import tpu as pltpu
from jax.sharding import Mesh
from jax.sharding import PartitionSpec as P

HEADS = 8
KV_HEADS = 4
HEAD_DIM = 256
STEP = 5


SOFT_CAP = 3.0
NORM_EPS = 1e-06
BETA_ONE = 0.9
BETA_TWO = 0.95
ADAM_EPS = 1e-08
MATRIX_RATE = 0.02
GAIN_RATE = 0.3
WEIGHT_DECAY = 0.1

PLANE = ("y", "x")
HEAD_AXES = ("y", "x", "core")
CTX = ("row", "y", "x", "core")
TENSOR = ("core", "fsdp")
EVERY = ("row", "y", "x", "core", "fsdp")


def rms_norm(values, gain_row):
    return values * lax.rsqrt(jnp.mean(values * values, -1, keepdims=True) + NORM_EPS) * gain_row


def norm_back(values, gain_row, grad_out):
    _, pull_back = jax.vjp(rms_norm, values, gain_row)
    grad_values, grad_gain = pull_back(grad_out)
    return (grad_values, jnp.sum(grad_gain.reshape(-1, grad_gain.shape[-1]), 0))


def gelu_tanh(values):
    return (
        0.5
        * values
        * (1.0 + jnp.tanh(0.7978845608028654 * (values + 0.044715 * values * values * values)))
    )


def gated_unit(gate_part, up_part):
    return gelu_tanh(gate_part) * up_part


def rotate(values, cos_table, sin_table):
    half_dim = values.shape[-1] // 2
    front_half = values[..., :half_dim]
    back_half = values[..., half_dim:]
    return jnp.concatenate(
        [
            front_half * cos_table - back_half * sin_table,
            back_half * cos_table + front_half * sin_table,
        ],
        -1,
    )


def rope_tables(positions, head_size):
    frequency = 10000.0 ** (-(jnp.arange(head_size // 2, dtype=jnp.float32) * 2.0) / head_size)
    turned = positions.astype(jnp.float32)[:, None] * frequency[None, :]
    return (jnp.cos(turned), jnp.sin(turned))


def positions_of(slot_table, row_total, block_size):
    row_ids = jnp.arange(row_total, dtype=jnp.int32)
    slot_ids = row_ids // block_size
    picked = jnp.sum(
        jnp.where(
            slot_ids[:, None] == jnp.arange(slot_table.shape[0], dtype=jnp.int32)[None, :],
            slot_table[None, :],
            0,
        ),
        1,
    )
    return picked * block_size + row_ids % block_size


def adamw(weight, moment_one, moment_two, gradient, rate, decay):
    first_new = BETA_ONE * moment_one + (1.0 - BETA_ONE) * gradient
    second_new = BETA_TWO * moment_two + (1.0 - BETA_TWO) * gradient * gradient
    step_size = (
        first_new
        / (1.0 - BETA_ONE**STEP)
        / (jnp.sqrt(second_new / (1.0 - BETA_TWO**STEP)) + ADAM_EPS)
    )
    return (first_new, second_new, weight - rate * (step_size + decay * weight))


def low(values):
    return values.astype(jnp.bfloat16)


def dot(left, right):
    return jnp.dot(left, right, preferred_element_type=jnp.float32)


def dot_t(left, right):
    return lax.dot_general(left, right, (((1,), (1,)), ((), ())), preferred_element_type=jnp.float32)


def t_dot(left, right):
    return lax.dot_general(left, right, (((0,), (0,)), ((), ())), preferred_element_type=jnp.float32)


def scores(query_rows, keys, row_positions, key_positions):
    raw = dot_t(query_rows, keys) * (HEAD_DIM ** (-0.5) / SOFT_CAP)
    tanh_part = jnp.tanh(raw)
    return jnp.where(key_positions <= row_positions, SOFT_CAP * tanh_part, -1e30), tanh_part


def attend_kernel(q_ref, k_ref, v_ref, row_ref, key_ref, out_ref, total_ref):
    capped, _ = scores(q_ref[...], k_ref[...], row_ref[...], key_ref[...])
    top_score = jnp.max(capped, -1, keepdims=True)
    exp_scores = jnp.exp(capped - top_score)
    exp_total = jnp.sum(exp_scores, -1, keepdims=True)
    probs = low(exp_scores * (1.0 / exp_total))
    out_ref[...] = low(dot(probs, v_ref[...]))
    total_ref[...] = top_score + jnp.log(exp_total)


def attend_back_kernel(
    core_ref, q_ref, k_ref, v_ref, grad_ref, total_ref, row_ref, key_ref, cos_ref, sin_ref,
    grad_q_ref, mine_ref, sent_ref, key_sum, value_sum,
):
    step = pl.program_id(0)
    query_rows, keys, grad_rows = q_ref[...], k_ref[...], grad_ref[...]
    capped, tanh_part = scores(query_rows, keys, row_ref[...], key_ref[...])
    probs = jnp.exp(capped - total_ref[...])
    grad_probs = dot_t(grad_rows, v_ref[...])
    inner_sum = jnp.sum(probs * grad_probs, -1, keepdims=True)
    grad_raw = low(probs * (grad_probs - inner_sum) * (1.0 - tanh_part * tanh_part))
    scale = HEAD_DIM ** (-0.5)
    grad_q = dot(grad_raw, keys) * scale
    grad_q_ref[...] = low(rotate(grad_q, cos_ref[...], -sin_ref[...]))
    key_terms = t_dot(grad_raw, query_rows)
    value_terms = t_dot(low(probs), grad_rows)

    @pl.when(step == 0)
    def _():
        key_sum[...] = key_terms
        value_sum[...] = value_terms

    @pl.when(step > 0)
    def _():
        key_sum[...] += key_terms
        value_sum[...] += value_terms

    @pl.when(step == pl.num_programs(0) - 1)
    def _():
        first = core_ref[0] == 0
        key_total, value_total = key_sum[...] * scale, value_sum[...]
        mine_ref[...] = jnp.where(first, key_total, value_total)
        sent_ref[...] = jnp.where(first, value_total, key_total)


def row_block(rows, columns):
    return pl.BlockSpec((rows, columns), lambda i: (i, 0))


def whole_block(rows, columns):
    return pl.BlockSpec((rows, columns), lambda i: (0, 0))


def kernel_params():
    return pltpu.CompilerParams(
        dimension_semantics=("arbitrary",), vmem_limit_bytes=48 * 1024 * 1024
    )


def attend(queries, keys, values, row_positions, key_positions):
    rows, columns = queries.shape
    length = keys.shape[0]
    block = min(rows, 256)
    return pl.pallas_call(
        attend_kernel,
        grid=(rows // block,),
        in_specs=[
            row_block(block, columns),
            whole_block(length, columns),
            whole_block(length, columns),
            row_block(block, 1),
            whole_block(1, length),
        ],
        out_specs=[row_block(block, columns), row_block(block, 1)],
        out_shape=[
            jax.ShapeDtypeStruct((rows, columns), jnp.bfloat16),
            jax.ShapeDtypeStruct((rows, 1), jnp.float32),
        ],
        compiler_params=kernel_params(),
        cost_estimate=pl.CostEstimate(
            flops=4 * rows * length * columns,
            bytes_accessed=4 * (rows + length) * columns,
            transcendentals=2 * rows * length,
        ),
        name="attend",
    )(queries, keys, values, row_positions[:, None], key_positions[None, :])


def attend_back(
    core_id, queries, keys, values, grads, totals, row_positions, key_positions, cos, sin
):
    rows, columns = queries.shape
    length = keys.shape[0]
    block = min(rows, 256)
    return pl.pallas_call(
        attend_back_kernel,
        grid=(rows // block,),
        in_specs=[
            pl.BlockSpec(memory_space=pltpu.SMEM),
            row_block(block, columns),
            whole_block(length, columns),
            whole_block(length, columns),
            row_block(block, columns),
            row_block(block, 1),
            row_block(block, 1),
            whole_block(1, length),
            row_block(block, columns // 2),
            row_block(block, columns // 2),
        ],
        out_specs=[
            row_block(block, columns),
            whole_block(length, columns),
            whole_block(length, columns),
        ],
        out_shape=[
            jax.ShapeDtypeStruct((rows, columns), jnp.bfloat16),
            jax.ShapeDtypeStruct((length, columns), jnp.float32),
            jax.ShapeDtypeStruct((length, columns), jnp.float32),
        ],
        scratch_shapes=[
            pltpu.VMEM((length, columns), jnp.float32),
            pltpu.VMEM((length, columns), jnp.float32),
        ],
        compiler_params=kernel_params(),
        cost_estimate=pl.CostEstimate(
            flops=10 * rows * length * columns,
            bytes_accessed=8 * (rows + 2 * length) * columns,
            transcendentals=2 * rows * length,
        ),
        name="attend_back",
    )(
        core_id.reshape(1),
        queries,
        keys,
        values,
        grads,
        totals,
        row_positions[:, None],
        key_positions[None, :],
        cos,
        sin,
    )


def gather_rows(piece, axes):
    return lax.all_gather(piece, axes, axis=0, tiled=True)


def scatter_rows(terms, axes):
    return lax.psum_scatter(terms, axes, scatter_dimension=0, tiled=True)


def exchange(piece, axis):
    return lax.ppermute(piece, axis, [(0, 1), (1, 0)])


def zero_after(*earlier):
    zero = jnp.float32(0)
    for array in earlier:
        first = lax.slice(array, (0,) * array.ndim, (1,) * array.ndim).reshape(())
        zero = zero + jnp.minimum(jnp.abs(first.astype(jnp.float32)), 0.0)
    return zero


def after(array, *earlier):
    return array + zero_after(*earlier).astype(array.dtype)


def in_order(mine, other, index, axis):
    return jnp.where(index == 0, jnp.stack([mine, other], axis), jnp.stack([other, mine], axis))


def gather_plane_near(block):
    half = block.shape[0] // 2
    return exchange(block[:half], "x"), exchange(block[half:], "y")


def gather_plane_far(block, near, zero=0.0):
    x_id, y_id = lax.axis_index("x"), lax.axis_index("y")
    half = block.shape[0] // 2
    upper_row = in_order(block[:half], near[0], x_id, 0)
    lower_column = in_order(block[half:], near[1], y_id, 0)
    late = jnp.asarray(zero, block.dtype)
    upper_all = in_order(upper_row + late, exchange(upper_row, "y"), y_id, 0)
    lower_all = in_order(lower_column + late, exchange(lower_column, "x"), x_id, 1)
    whole = jnp.concatenate([upper_all, lower_all], 2)
    return whole.reshape(4 * block.shape[0], block.shape[1])


def gather_heads(block, earlier):
    plane = gather_plane_far(block, gather_plane_near(block), zero_after(earlier))
    both = in_order(
        plane.reshape((HEADS // 2,) + block.shape),
        exchange(plane, "core").reshape((HEADS // 2,) + block.shape),
        lax.axis_index("core"),
        1,
    )
    return both.reshape(HEADS * block.shape[0], block.shape[1])


def scatter_plane_far(terms):
    x_id, y_id = lax.axis_index("x"), lax.axis_index("y")
    rows, columns = terms.shape[0] // 4, terms.shape[1]
    half = rows // 2
    start = (2 * (1 - y_id) + 1 - x_id) * rows
    upper = lax.dynamic_slice(terms, (start, 0), (half, columns))
    lower = lax.dynamic_slice(terms, (start + half, 0), (half, columns))
    return exchange(upper, "x"), exchange(lower, "y")


def scatter_plane_near(terms, far):
    x_id, y_id = lax.axis_index("x"), lax.axis_index("y")
    rows, columns = terms.shape[0] // 4, terms.shape[1]
    half = rows // 2

    def part(y_at, x_at, first):
        start = (2 * y_at + x_at) * rows + first
        return lax.dynamic_slice(terms, (start, 0), (half, columns))

    def add(left, right):
        return low(left.astype(jnp.float32) + right.astype(jnp.float32))

    upper_far, lower_far = far
    to_y = jnp.concatenate([add(part(1 - y_id, x_id, 0), upper_far), part(1 - y_id, x_id, half)], 0)
    to_x = jnp.concatenate([part(y_id, 1 - x_id, 0), add(part(y_id, 1 - x_id, half), lower_far)], 0)
    return to_y, to_x


def scatter_plane_sum(terms, from_y, from_x):
    x_id, y_id = lax.axis_index("x"), lax.axis_index("y")
    rows, columns = terms.shape[0] // 4, terms.shape[1]
    mine = lax.dynamic_slice(terms, ((2 * y_id + x_id) * rows, 0), (rows, columns))
    return mine.astype(jnp.float32) + from_y.astype(jnp.float32) + from_x.astype(jnp.float32)


def scatter_plane(terms):
    to_y, to_x = scatter_plane_near(terms, scatter_plane_far(terms))
    return scatter_plane_sum(terms, exchange(to_y, "y"), exchange(to_x, "x"))


def my_half(first, second):
    return jnp.where(lax.axis_index("core") == 0, first, second)


def tensor_terms(terms, zero=0.0):
    half = terms.shape[0] // 2
    came = exchange(my_half(terms[half:], terms[:half]), "core")
    mine = my_half(terms[:half], terms[half:])
    return low(mine.astype(jnp.float32) + (came.astype(jnp.float32) + zero))


def head_terms(terms):
    rows, width = terms.shape
    blocks = terms.reshape(HEADS // 2, 2, rows // HEADS, width)
    came = exchange(my_half(blocks[:, 1], blocks[:, 0]), "core")
    mine = my_half(blocks[:, 0], blocks[:, 1])
    return low(mine.astype(jnp.float32) + came.astype(jnp.float32)).reshape(rows // 2, width)


def over_fsdp(terms, fsdp_count):
    blocks = terms.reshape(fsdp_count, terms.shape[0] // fsdp_count, terms.shape[1])
    return lax.all_to_all(blocks, "fsdp", split_axis=0, concat_axis=0, tiled=True)


def columns_out(weight_piece, axes, parts):
    rows = weight_piece.shape[0]
    blocks = jnp.transpose(weight_piece.reshape(rows, parts, -1), (1, 0, 2))
    return lax.all_to_all(blocks, axes, split_axis=0, concat_axis=0, tiled=True).reshape(
        parts * rows, -1
    )


def blocks_back(grad_piece, axes, parts):
    blocks = grad_piece.reshape(parts, -1, grad_piece.shape[1])
    return lax.all_to_all(blocks, axes, split_axis=0, concat_axis=0, tiled=True)


def side_by_side(blocks):
    parts, rows, columns = blocks.shape
    return jnp.swapaxes(blocks, 0, 1).reshape(rows, parts * columns).astype(jnp.float32)


def per_device(
    tokens,
    cotangent,
    block_order,
    w_qkv,
    w_out,
    w_gate_up,
    w_down,
    norm_gains,
    first_qkv,
    first_out,
    first_gate_up,
    first_down,
    first_gains,
    second_qkv,
    second_out,
    second_gate_up,
    second_down,
    second_gains,
):
    row_count = tokens.shape[1]
    block_size = row_count // 2
    row_parts = lax.axis_size("row")
    fsdp_count = lax.axis_size("fsdp")
    core_id = lax.axis_index("core")
    row_id = lax.axis_index("row")
    seq_length = row_count * row_parts * HEADS
    query_rows = row_count * HEADS
    own_rows = w_qkv.shape[0]
    width = tokens.shape[2]
    q_width = HEADS * HEAD_DIM
    kv_width = KV_HEADS * HEAD_DIM
    ff_width = w_down.shape[1]
    tensor_parts = 2 * fsdp_count
    ff_own = ff_width // tensor_parts
    scale = HEAD_DIM ** (-0.5)

    gate_up_mine = columns_out(
        jnp.concatenate(
            [
                low(w_gate_up[:, :ff_width]).reshape(own_rows, tensor_parts, ff_own),
                low(w_gate_up[:, ff_width:]).reshape(own_rows, tensor_parts, ff_own),
            ],
            2,
        ),
        TENSOR,
        tensor_parts,
    )
    own_gate_up = gather_rows(gate_up_mine, ("row",) + PLANE)
    seq_tokens = gather_rows(tokens[0], CTX)

    def to_heads(pieces):
        copies = jnp.broadcast_to(
            pieces[None, :, None], (row_parts, HEADS, fsdp_count) + pieces.shape[1:]
        ).reshape((-1,) + pieces.shape[1:])
        return lax.all_to_all(copies, EVERY, split_axis=0, concat_axis=0, tiled=True)

    q_cols = low(w_qkv[:, :q_width]).reshape(own_rows, HEADS, HEAD_DIM)
    k_cols = low(w_qkv[:, q_width : q_width + kv_width]).reshape(own_rows, KV_HEADS, 1, HEAD_DIM)
    v_cols = low(w_qkv[:, q_width + kv_width :]).reshape(own_rows, KV_HEADS, 1, HEAD_DIM)
    kv_cols = jnp.concatenate([k_cols, v_cols], 2).reshape(own_rows, HEADS, HEAD_DIM)
    qkv_cols = jnp.concatenate([q_cols, kv_cols], 2)
    gain_piece = jnp.pad(
        low(norm_gains).reshape(1, 1, 4 * own_rows),
        ((0, HEADS - 1), (0, 7), (0, 2 * HEAD_DIM - 4 * own_rows)),
        mode="edge",
    )
    pieces = jnp.concatenate([jnp.swapaxes(qkv_cols, 0, 1), gain_piece], 1)
    received = to_heads(after(pieces, gate_up_mine))
    head_qkv = received[:, :own_rows].reshape(width, 2 * HEAD_DIM)
    gains = (
        jnp.swapaxes(received[:, own_rows, : 4 * own_rows].reshape(-1, 4, own_rows), 0, 1)
        .reshape(4, width)
        .astype(jnp.float32)
    )
    out_pieces = jnp.swapaxes(low(w_out).reshape(own_rows, HEADS, HEAD_DIM), 0, 1)
    head_out = to_heads(after(out_pieces, received)).reshape(width, HEAD_DIM)

    down_mine = columns_out(after(low(w_down), head_out), TENSOR, tensor_parts)

    key_positions = positions_of(block_order, seq_length, block_size)
    cos_table, sin_table = rope_tables(key_positions, HEAD_DIM)
    first_row = row_id * query_rows

    def query_part(array):
        if row_parts == 1:
            return array
        return lax.dynamic_slice_in_dim(array, first_row, query_rows, 0)

    query_cos, query_sin = query_part(cos_table), query_part(sin_table)
    row_positions = query_part(key_positions)

    inputs = tokens[0].astype(jnp.float32)
    normed_one = low(rms_norm(seq_tokens.astype(jnp.float32), gains[0]))
    normed_query = query_part(normed_one)
    queries = low(rotate(dot(normed_query, head_qkv[:, :HEAD_DIM]), query_cos, query_sin))
    kv_raw = dot(normed_one, head_qkv[:, HEAD_DIM:])
    kv_mine = low(jnp.where(core_id == 0, rotate(kv_raw, cos_table, sin_table), kv_raw))
    kv_other = exchange(kv_mine, "core")
    keys = jnp.where(core_id == 0, kv_mine, kv_other)
    values = jnp.where(core_id == 0, kv_other, kv_mine)
    attended, log_total = attend(queries, keys, values, row_positions, key_positions)
    branch = scatter_plane(head_terms(low(dot_t(attended, head_out))))
    hidden_in = after(inputs, own_gate_up, down_mine) + rms_norm(branch, gains[1])

    part_rows = row_count // 2

    def part(array, index):
        return array[index * part_rows : (index + 1) * part_rows]

    normed_two_mine = low(rms_norm(hidden_in, gains[2]))
    down_mine = after(down_mine, normed_two_mine)
    down_near = gather_plane_near(down_mine)
    upstream = cotangent[0].astype(jnp.float32)

    def forward_part(gate_up, own_down, zero):
        activated = low(gated_unit(gate_up[:, :ff_own], gate_up[:, ff_own:]))
        terms = tensor_terms(low(dot_t(activated, own_down)), zero)
        return activated, terms, over_fsdp(terms, fsdp_count)

    def factors_of(gate_up, zero):
        gate_part, up_part = gate_up[:, :ff_own] + zero, gate_up[:, ff_own:] + zero
        _, pull_back = jax.vjp(gated_unit, gate_part, up_part)
        factors = pull_back(jnp.ones_like(gate_part))
        return lax.optimization_barrier(tuple(low(factor) for factor in factors))

    def turn_part(index, pieces, zero):
        lowered = jnp.sum(pieces.astype(jnp.float32), 0)
        output = low(part(hidden_in, index) + rms_norm(lowered, gains[3]))
        grad_lowered, gain = norm_back(lowered, gains[3], part(upstream, index))
        return output, low(grad_lowered + zero), gain

    def backward_part(grad_lowered, factors, zero, terms_zero):
        grad_activated = dot(grad_lowered, own_down) + zero
        grad_gate_up = lax.optimization_barrier(
            low(jnp.concatenate([grad_activated * factors[0], grad_activated * factors[1]], 1))
        )
        terms = tensor_terms(low(dot_t(grad_gate_up, own_gate_up)), terms_zero)
        return grad_gate_up, terms, over_fsdp(terms, fsdp_count)

    def both(first, second, zero=0.0):
        whole = jnp.concatenate(lax.optimization_barrier((first, second)), 0)
        return lax.optimization_barrier(whole + jnp.asarray(zero, whole.dtype))

    rows_one = gather_rows(part(normed_two_mine, 0), TENSOR)
    rows_two = gather_rows(part(normed_two_mine, 1), TENSOR)
    product_one = dot(rows_one, own_gate_up)
    own_down = gather_plane_far(down_mine, down_near, zero_after(product_one))
    if row_parts > 1:
        own_down = gather_rows(own_down, "row")
    activated_one, lowered_terms, pieces_one = forward_part(product_one, own_down, 0.0)
    output_one, sent_one, gain_three_one = turn_part(0, pieces_one, 0.0)
    lowered_one = gather_rows(sent_one, TENSOR)
    product_two = dot(after(rows_two, lowered_terms), own_gate_up)
    activated_two, lowered_terms, pieces_two = forward_part(
        product_two, own_down, zero_after(sent_one)
    )
    later = zero_after(lowered_terms)
    factors_one, factors_two = factors_of(product_one, later), factors_of(product_two, later)
    normed_two = both(rows_one, rows_two, later)
    activated = both(activated_one, activated_two, later)
    output_two, sent_two, gain_three_two = turn_part(
        1, pieces_two, zero_after(normed_two, activated, *factors_one, *factors_two)
    )
    lowered_two = gather_rows(sent_two, TENSOR)
    output = jnp.concatenate([output_one, output_two], 0)[None]
    gain_three = gain_three_one + gain_three_two
    gate_up_one, terms_one, back_one = backward_part(
        lowered_one, factors_one, zero_after(sent_two), 0.0
    )
    normed_two_one = jnp.sum(back_one.astype(jnp.float32), 0)
    grad_lowered = both(lowered_one, lowered_two, zero_after(terms_one))
    term_down = low(t_dot(grad_lowered, activated))
    gate_up_two, terms_two, back_two = backward_part(
        lowered_two, factors_two, zero_after(term_down), zero_after(normed_two_one)
    )

    plane_down = scatter_rows(term_down, ("row",) + PLANE)
    grad_gate_up = both(gate_up_one, gate_up_two)
    term_gate = low(t_dot(normed_two, after(grad_gate_up[:, :ff_own], terms_two)))
    plane_gate = scatter_rows(term_gate, ("row",) + PLANE)
    term_up = low(t_dot(normed_two, after(grad_gate_up[:, ff_own:], term_gate)))
    plane_up = scatter_rows(term_up, ("row",) + PLANE)
    normed_two_two = jnp.sum(after(back_two, term_up).astype(jnp.float32), 0)
    grad_normed_two = jnp.concatenate([normed_two_one, normed_two_two], 0)

    grad_hidden_part, gain_two = norm_back(hidden_in, gains[2], grad_normed_two)
    grad_hidden = upstream + grad_hidden_part
    grad_branch, gain_one = norm_back(branch, gains[1], grad_hidden)
    grad_branch_mine = low(grad_branch)
    blocks_down = blocks_back(after(plane_down, grad_normed_two), TENSOR, tensor_parts)
    grad_branch = gather_heads(grad_branch_mine, blocks_down)
    blocks_gate = blocks_back(plane_gate, TENSOR, tensor_parts)

    grad_attended = low(dot(grad_branch, head_out))
    query_back, kv_terms, kv_sent = attend_back(
        core_id,
        queries,
        keys,
        values,
        grad_attended,
        log_total,
        row_positions,
        key_positions,
        query_cos,
        query_sin,
    )
    kv_terms = kv_terms + exchange(kv_sent, "core")
    if row_parts > 1:
        kv_terms = scatter_rows(kv_terms, "row")
    kv_back = jnp.where(core_id == 0, rotate(kv_terms, query_cos, -query_sin), kv_terms)
    grad_projected = jnp.concatenate([query_back, low(kv_back + zero_after(blocks_gate))], 1)
    grad_normed_one = scatter_plane(head_terms(low(dot_t(grad_projected, head_qkv))))
    grad_input_part, gain_zero = norm_back(inputs, gains[0], grad_normed_one)
    token_grad = low(grad_hidden + grad_input_part)[None]

    def to_owners(term):
        blocks = term.reshape(row_parts * HEADS * fsdp_count, -1, term.shape[1])
        return lax.all_to_all(blocks, EVERY, split_axis=0, concat_axis=0, tiled=True)

    def head_grad(pieces):
        pieces = pieces.reshape((row_parts, HEADS, fsdp_count) + pieces.shape[1:])
        return jnp.swapaxes(jnp.sum(pieces.astype(jnp.float32), (0, 2)), 0, 1)

    qkv_term = low(t_dot(normed_query, grad_projected))
    if row_parts > 1:
        qkv_term = scatter_rows(qkv_term, "row")
    by_owner = jnp.swapaxes(qkv_term.reshape(HEADS, fsdp_count, own_rows, -1), 0, 1)
    qkv_mine = scatter_rows(by_owner.reshape(qkv_term.shape), "fsdp")
    out_term = lax.optimization_barrier(low(t_dot(grad_branch, attended)))
    out_pieces = to_owners(out_term)
    blocks_up = blocks_back(after(plane_up, qkv_term), TENSOR, tensor_parts)
    qkv_blocks = blocks_back(qkv_mine, HEAD_AXES, HEADS)
    sum_qkv = jnp.swapaxes(qkv_blocks, 0, 1).astype(jnp.float32)
    gain_terms = jnp.stack([gain_zero, gain_one, gain_two, gain_three], 0)
    gain_terms = jnp.swapaxes(gain_terms.reshape(4, -1, own_rows), 0, 1)
    gain_pieces = lax.all_to_all(
        after(gain_terms, qkv_blocks), EVERY, split_axis=0, concat_axis=0, tiled=True
    )
    grad_gains = jnp.sum(gain_pieces, 0)
    grad_out = head_grad(out_pieces).reshape(own_rows, q_width)
    kv_sum = sum_qkv[:, :, HEAD_DIM:].reshape(own_rows, KV_HEADS, 2, HEAD_DIM)
    grad_qkv = jnp.concatenate(
        [
            sum_qkv[:, :, :HEAD_DIM].reshape(own_rows, q_width),
            kv_sum[:, :, 0].reshape(own_rows, kv_width),
            kv_sum[:, :, 1].reshape(own_rows, kv_width),
        ],
        1,
    )
    grad_down = side_by_side(blocks_down)
    grad_gate_up_w = jnp.concatenate(
        [after(side_by_side(blocks_gate), qkv_mine), side_by_side(blocks_up)], 1
    )
    moment_qkv, square_qkv, new_qkv = adamw(
        w_qkv, first_qkv, second_qkv, grad_qkv, MATRIX_RATE, WEIGHT_DECAY
    )
    moment_out, square_out, new_out = adamw(
        w_out, first_out, second_out, grad_out, MATRIX_RATE, WEIGHT_DECAY
    )
    moment_gate_up, square_gate_up, new_gate_up = adamw(
        w_gate_up, first_gate_up, second_gate_up, grad_gate_up_w, MATRIX_RATE, WEIGHT_DECAY
    )
    moment_down, square_down, new_down = adamw(
        w_down, first_down, second_down, grad_down, MATRIX_RATE, WEIGHT_DECAY
    )
    moment_gains, square_gains, new_gains = adamw(
        norm_gains, first_gains, second_gains, grad_gains, GAIN_RATE, 0.0
    )
    return (
        output,
        token_grad,
        moment_qkv,
        moment_out,
        moment_gate_up,
        moment_down,
        moment_gains,
        square_qkv,
        square_out,
        square_gate_up,
        square_down,
        square_gains,
        new_qkv,
        new_out,
        new_gate_up,
        new_down,
        new_gains,
    )


def solution(mesh):
    ctx_count, fsdp_count = mesh.shape["ctx"], mesh.shape["fsdp"]
    fine_mesh = Mesh(mesh.devices.reshape(ctx_count // HEADS, 2, 2, 2, fsdp_count), EVERY)
    rows = P("fsdp", CTX, None)
    weight = P(EVERY, None)
    gain = P(None, EVERY)
    weights = (weight, weight, weight, weight, gain)
    return jax.shard_map(
        per_device,
        mesh=fine_mesh,
        in_specs=(rows, rows, P()) + weights * 3,
        out_specs=(rows, rows) + weights * 3,
        check_vma=False,
    )
```

```python
import jax
import jax.numpy as jnp
from jax import lax
from jax.experimental import pallas as pl
from jax.experimental.pallas import tpu as pltpu
from jax.sharding import Mesh
from jax.sharding import PartitionSpec as P

HEADS = 8
KV_HEADS = 4
HEAD_DIM = 256
STEP = 5


SOFT_CAP = 3.0
NORM_EPS = 1e-06
BETA_ONE = 0.9
BETA_TWO = 0.95
ADAM_EPS = 1e-08
MATRIX_RATE = 0.02
GAIN_RATE = 0.3
WEIGHT_DECAY = 0.1

PLANE = ("y", "x")
HEAD_AXES = ("y", "x", "core")
CTX = ("row", "y", "x", "core")
TENSOR = ("core", "fsdp")
EVERY = ("row", "y", "x", "core", "fsdp")


def rms_norm(values, gain_row):
    return values * lax.rsqrt(jnp.mean(values * values, -1, keepdims=True) + NORM_EPS) * gain_row


def norm_back(values, gain_row, grad_out):
    _, pull_back = jax.vjp(rms_norm, values, gain_row)
    grad_values, grad_gain = pull_back(grad_out)
    return (grad_values, jnp.sum(grad_gain.reshape(-1, grad_gain.shape[-1]), 0))


def gelu_tanh(values):
    return (
        0.5
        * values
        * (1.0 + jnp.tanh(0.7978845608028654 * (values + 0.044715 * values * values * values)))
    )


def gated_unit(gate_part, up_part):
    return gelu_tanh(gate_part) * up_part


def rotate(values, cos_table, sin_table):
    half_dim = values.shape[-1] // 2
    front_half = values[..., :half_dim]
    back_half = values[..., half_dim:]
    return jnp.concatenate(
        [
            front_half * cos_table - back_half * sin_table,
            back_half * cos_table + front_half * sin_table,
        ],
        -1,
    )


def rope_tables(positions, head_size):
    frequency = 10000.0 ** (-(jnp.arange(head_size // 2, dtype=jnp.float32) * 2.0) / head_size)
    turned = positions.astype(jnp.float32)[:, None] * frequency[None, :]
    return (jnp.cos(turned), jnp.sin(turned))


def positions_of(slot_table, row_total, block_size):
    row_ids = jnp.arange(row_total, dtype=jnp.int32)
    slot_ids = row_ids // block_size
    picked = jnp.sum(
        jnp.where(
            slot_ids[:, None] == jnp.arange(slot_table.shape[0], dtype=jnp.int32)[None, :],
            slot_table[None, :],
            0,
        ),
        1,
    )
    return picked * block_size + row_ids % block_size


def adamw(weight, moment_one, moment_two, gradient, rate, decay):
    first_new = BETA_ONE * moment_one + (1.0 - BETA_ONE) * gradient
    second_new = BETA_TWO * moment_two + (1.0 - BETA_TWO) * gradient * gradient
    step_size = (
        first_new
        / (1.0 - BETA_ONE**STEP)
        / (jnp.sqrt(second_new / (1.0 - BETA_TWO**STEP)) + ADAM_EPS)
    )
    return (first_new, second_new, weight - rate * (step_size + decay * weight))


def low(values):
    return values.astype(jnp.bfloat16)


def dot(left, right):
    return jnp.dot(left, right, preferred_element_type=jnp.float32)


def dot_t(left, right):
    return lax.dot_general(left, right, (((1,), (1,)), ((), ())), preferred_element_type=jnp.float32)


def t_dot(left, right):
    return lax.dot_general(left, right, (((0,), (0,)), ((), ())), preferred_element_type=jnp.float32)


def scores(query_rows, keys, row_positions, key_positions):
    raw = dot_t(query_rows, keys) * (HEAD_DIM ** (-0.5) / SOFT_CAP)
    tanh_part = jnp.tanh(raw)
    return jnp.where(key_positions <= row_positions, SOFT_CAP * tanh_part, -1e30), tanh_part


def attend_kernel(q_ref, k_ref, v_ref, row_ref, key_ref, out_ref, total_ref):
    capped, _ = scores(q_ref[...], k_ref[...], row_ref[...], key_ref[...])
    top_score = jnp.max(capped, -1, keepdims=True)
    exp_scores = jnp.exp(capped - top_score)
    exp_total = jnp.sum(exp_scores, -1, keepdims=True)
    probs = low(exp_scores * (1.0 / exp_total))
    out_ref[...] = low(dot(probs, v_ref[...]))
    total_ref[...] = top_score + jnp.log(exp_total)


def attend_back_kernel(
    core_ref, q_ref, k_ref, v_ref, grad_ref, total_ref, row_ref, key_ref, cos_ref, sin_ref,
    grad_q_ref, mine_ref, sent_ref, key_sum, value_sum,
):
    step = pl.program_id(0)
    query_rows, keys, grad_rows = q_ref[...], k_ref[...], grad_ref[...]
    capped, tanh_part = scores(query_rows, keys, row_ref[...], key_ref[...])
    probs = jnp.exp(capped - total_ref[...])
    grad_probs = dot_t(grad_rows, v_ref[...])
    inner_sum = jnp.sum(probs * grad_probs, -1, keepdims=True)
    grad_raw = low(probs * (grad_probs - inner_sum) * (1.0 - tanh_part * tanh_part))
    scale = HEAD_DIM ** (-0.5)
    grad_q = dot(grad_raw, keys) * scale
    grad_q_ref[...] = low(rotate(grad_q, cos_ref[...], -sin_ref[...]))
    key_terms = t_dot(grad_raw, query_rows)
    value_terms = t_dot(low(probs), grad_rows)

    @pl.when(step == 0)
    def _():
        key_sum[...] = key_terms
        value_sum[...] = value_terms

    @pl.when(step > 0)
    def _():
        key_sum[...] += key_terms
        value_sum[...] += value_terms

    @pl.when(step == pl.num_programs(0) - 1)
    def _():
        first = core_ref[0] == 0
        key_total, value_total = key_sum[...] * scale, value_sum[...]
        mine_ref[...] = jnp.where(first, key_total, value_total)
        sent_ref[...] = jnp.where(first, value_total, key_total)


def row_block(rows, columns):
    return pl.BlockSpec((rows, columns), lambda i: (i, 0))


def whole_block(rows, columns):
    return pl.BlockSpec((rows, columns), lambda i: (0, 0))


def kernel_params():
    return pltpu.CompilerParams(
        dimension_semantics=("arbitrary",), vmem_limit_bytes=48 * 1024 * 1024
    )


def attend(queries, keys, values, row_positions, key_positions):
    rows, columns = queries.shape
    length = keys.shape[0]
    block = min(rows, 256)
    return pl.pallas_call(
        attend_kernel,
        grid=(rows // block,),
        in_specs=[
            row_block(block, columns),
            whole_block(length, columns),
            whole_block(length, columns),
            row_block(block, 1),
            whole_block(1, length),
        ],
        out_specs=[row_block(block, columns), row_block(block, 1)],
        out_shape=[
            jax.ShapeDtypeStruct((rows, columns), jnp.bfloat16),
            jax.ShapeDtypeStruct((rows, 1), jnp.float32),
        ],
        compiler_params=kernel_params(),
        cost_estimate=pl.CostEstimate(
            flops=4 * rows * length * columns,
            bytes_accessed=4 * (rows + length) * columns,
            transcendentals=2 * rows * length,
        ),
        name="attend",
    )(queries, keys, values, row_positions[:, None], key_positions[None, :])


def attend_back(
    core_id, queries, keys, values, grads, totals, row_positions, key_positions, cos, sin
):
    rows, columns = queries.shape
    length = keys.shape[0]
    block = min(rows, 256)
    return pl.pallas_call(
        attend_back_kernel,
        grid=(rows // block,),
        in_specs=[
            pl.BlockSpec(memory_space=pltpu.SMEM),
            row_block(block, columns),
            whole_block(length, columns),
            whole_block(length, columns),
            row_block(block, columns),
            row_block(block, 1),
            row_block(block, 1),
            whole_block(1, length),
            row_block(block, columns // 2),
            row_block(block, columns // 2),
        ],
        out_specs=[
            row_block(block, columns),
            whole_block(length, columns),
            whole_block(length, columns),
        ],
        out_shape=[
            jax.ShapeDtypeStruct((rows, columns), jnp.bfloat16),
            jax.ShapeDtypeStruct((length, columns), jnp.float32),
            jax.ShapeDtypeStruct((length, columns), jnp.float32),
        ],
        scratch_shapes=[
            pltpu.VMEM((length, columns), jnp.float32),
            pltpu.VMEM((length, columns), jnp.float32),
        ],
        compiler_params=kernel_params(),
        cost_estimate=pl.CostEstimate(
            flops=10 * rows * length * columns,
            bytes_accessed=8 * (rows + 2 * length) * columns,
            transcendentals=2 * rows * length,
        ),
        name="attend_back",
    )(
        core_id.reshape(1),
        queries,
        keys,
        values,
        grads,
        totals,
        row_positions[:, None],
        key_positions[None, :],
        cos,
        sin,
    )


def gather_rows(piece, axes):
    return lax.all_gather(piece, axes, axis=0, tiled=True)


def scatter_rows(terms, axes):
    return lax.psum_scatter(terms, axes, scatter_dimension=0, tiled=True)


def exchange(piece, axis):
    return lax.ppermute(piece, axis, [(0, 1), (1, 0)])


def zero_after(*earlier):
    zero = jnp.float32(0)
    for array in earlier:
        first = lax.slice(array, (0,) * array.ndim, (1,) * array.ndim).reshape(())
        zero = zero + jnp.minimum(jnp.abs(first.astype(jnp.float32)), 0.0)
    return zero


def after(array, *earlier):
    return array + zero_after(*earlier).astype(array.dtype)


def in_order(mine, other, index, axis):
    return jnp.where(index == 0, jnp.stack([mine, other], axis), jnp.stack([other, mine], axis))


def gather_plane_near(block):
    half = block.shape[0] // 2
    return exchange(block[:half], "x"), exchange(block[half:], "y")


def gather_plane_far(block, near, zero=0.0):
    x_id, y_id = lax.axis_index("x"), lax.axis_index("y")
    half = block.shape[0] // 2
    upper_row = in_order(block[:half], near[0], x_id, 0)
    lower_column = in_order(block[half:], near[1], y_id, 0)
    late = jnp.asarray(zero, block.dtype)
    upper_all = in_order(upper_row + late, exchange(upper_row, "y"), y_id, 0)
    lower_all = in_order(lower_column + late, exchange(lower_column, "x"), x_id, 1)
    whole = jnp.concatenate([upper_all, lower_all], 2)
    return whole.reshape(4 * block.shape[0], block.shape[1])


def gather_heads(block, earlier):
    plane = gather_plane_far(block, gather_plane_near(block), zero_after(earlier))
    both = in_order(
        plane.reshape((HEADS // 2,) + block.shape),
        exchange(plane, "core").reshape((HEADS // 2,) + block.shape),
        lax.axis_index("core"),
        1,
    )
    return both.reshape(HEADS * block.shape[0], block.shape[1])


def scatter_plane_far(terms):
    x_id, y_id = lax.axis_index("x"), lax.axis_index("y")
    rows, columns = terms.shape[0] // 4, terms.shape[1]
    half = rows // 2
    start = (2 * (1 - y_id) + 1 - x_id) * rows
    upper = lax.dynamic_slice(terms, (start, 0), (half, columns))
    lower = lax.dynamic_slice(terms, (start + half, 0), (half, columns))
    return exchange(upper, "x"), exchange(lower, "y")


def scatter_plane_near(terms, far):
    x_id, y_id = lax.axis_index("x"), lax.axis_index("y")
    rows, columns = terms.shape[0] // 4, terms.shape[1]
    half = rows // 2

    def part(y_at, x_at, first):
        start = (2 * y_at + x_at) * rows + first
        return lax.dynamic_slice(terms, (start, 0), (half, columns))

    def add(left, right):
        return low(left.astype(jnp.float32) + right.astype(jnp.float32))

    upper_far, lower_far = far
    to_y = jnp.concatenate([add(part(1 - y_id, x_id, 0), upper_far), part(1 - y_id, x_id, half)], 0)
    to_x = jnp.concatenate([part(y_id, 1 - x_id, 0), add(part(y_id, 1 - x_id, half), lower_far)], 0)
    return to_y, to_x


def scatter_plane_sum(terms, from_y, from_x):
    x_id, y_id = lax.axis_index("x"), lax.axis_index("y")
    rows, columns = terms.shape[0] // 4, terms.shape[1]
    mine = lax.dynamic_slice(terms, ((2 * y_id + x_id) * rows, 0), (rows, columns))
    return mine.astype(jnp.float32) + from_y.astype(jnp.float32) + from_x.astype(jnp.float32)


def scatter_plane(terms):
    to_y, to_x = scatter_plane_near(terms, scatter_plane_far(terms))
    return scatter_plane_sum(terms, exchange(to_y, "y"), exchange(to_x, "x"))


def my_half(first, second):
    return jnp.where(lax.axis_index("core") == 0, first, second)


def tensor_terms(terms, zero=0.0):
    half = terms.shape[0] // 2
    sent = my_half(terms[half:], terms[:half])
    came = exchange(sent, "core")
    mine = my_half(terms[:half], terms[half:])
    return low(mine.astype(jnp.float32) + (came.astype(jnp.float32) + zero)), sent


def head_terms(terms):
    rows, width = terms.shape
    blocks = terms.reshape(HEADS // 2, 2, rows // HEADS, width)
    came = exchange(my_half(blocks[:, 1], blocks[:, 0]), "core")
    mine = my_half(blocks[:, 0], blocks[:, 1])
    return low(mine.astype(jnp.float32) + came.astype(jnp.float32)).reshape(rows // 2, width)


def over_fsdp(terms, fsdp_count):
    blocks = terms.reshape(fsdp_count, terms.shape[0] // fsdp_count, terms.shape[1])
    return lax.all_to_all(blocks, "fsdp", split_axis=0, concat_axis=0, tiled=True)


def columns_out(weight_piece, axes, parts):
    rows = weight_piece.shape[0]
    blocks = jnp.transpose(weight_piece.reshape(rows, parts, -1), (1, 0, 2))
    return lax.all_to_all(blocks, axes, split_axis=0, concat_axis=0, tiled=True).reshape(
        parts * rows, -1
    )


def blocks_back(grad_piece, axes, parts):
    blocks = grad_piece.reshape(parts, -1, grad_piece.shape[1])
    return lax.all_to_all(blocks, axes, split_axis=0, concat_axis=0, tiled=True)


def side_by_side(blocks):
    parts, rows, columns = blocks.shape
    return jnp.swapaxes(blocks, 0, 1).reshape(rows, parts * columns).astype(jnp.float32)


def per_device(
    tokens,
    cotangent,
    block_order,
    w_qkv,
    w_out,
    w_gate_up,
    w_down,
    norm_gains,
    first_qkv,
    first_out,
    first_gate_up,
    first_down,
    first_gains,
    second_qkv,
    second_out,
    second_gate_up,
    second_down,
    second_gains,
):
    row_count = tokens.shape[1]
    block_size = row_count // 2
    row_parts = lax.axis_size("row")
    fsdp_count = lax.axis_size("fsdp")
    core_id = lax.axis_index("core")
    row_id = lax.axis_index("row")
    seq_length = row_count * row_parts * HEADS
    query_rows = row_count * HEADS
    own_rows = w_qkv.shape[0]
    width = tokens.shape[2]
    q_width = HEADS * HEAD_DIM
    kv_width = KV_HEADS * HEAD_DIM
    ff_width = w_down.shape[1]
    tensor_parts = 2 * fsdp_count
    ff_own = ff_width // tensor_parts
    scale = HEAD_DIM ** (-0.5)

    gate_up_mine = columns_out(
        jnp.concatenate(
            [
                low(w_gate_up[:, :ff_width]).reshape(own_rows, tensor_parts, ff_own),
                low(w_gate_up[:, ff_width:]).reshape(own_rows, tensor_parts, ff_own),
            ],
            2,
        ),
        TENSOR,
        tensor_parts,
    )
    own_gate_up = gather_rows(gate_up_mine, ("row",) + PLANE)
    seq_tokens = gather_rows(tokens[0], CTX)

    def to_heads(pieces):
        copies = jnp.broadcast_to(
            pieces[None, :, None], (row_parts, HEADS, fsdp_count) + pieces.shape[1:]
        ).reshape((-1,) + pieces.shape[1:])
        return lax.all_to_all(copies, EVERY, split_axis=0, concat_axis=0, tiled=True)

    q_cols = low(w_qkv[:, :q_width]).reshape(own_rows, HEADS, HEAD_DIM)
    k_cols = low(w_qkv[:, q_width : q_width + kv_width]).reshape(own_rows, KV_HEADS, 1, HEAD_DIM)
    v_cols = low(w_qkv[:, q_width + kv_width :]).reshape(own_rows, KV_HEADS, 1, HEAD_DIM)
    kv_cols = jnp.concatenate([k_cols, v_cols], 2).reshape(own_rows, HEADS, HEAD_DIM)
    qkv_cols = jnp.concatenate([q_cols, kv_cols], 2)
    gain_piece = jnp.pad(
        low(norm_gains).reshape(1, 1, 4 * own_rows),
        ((0, HEADS - 1), (0, 7), (0, 2 * HEAD_DIM - 4 * own_rows)),
        mode="edge",
    )
    pieces = jnp.concatenate([jnp.swapaxes(qkv_cols, 0, 1), gain_piece], 1)
    received = to_heads(after(pieces, gate_up_mine))
    head_qkv = received[:, :own_rows].reshape(width, 2 * HEAD_DIM)
    gains = (
        jnp.swapaxes(received[:, own_rows, : 4 * own_rows].reshape(-1, 4, own_rows), 0, 1)
        .reshape(4, width)
        .astype(jnp.float32)
    )
    out_pieces = jnp.swapaxes(low(w_out).reshape(own_rows, HEADS, HEAD_DIM), 0, 1)
    head_out = to_heads(after(out_pieces, received)).reshape(width, HEAD_DIM)

    down_mine = columns_out(after(low(w_down), head_out), TENSOR, tensor_parts)

    key_positions = positions_of(block_order, seq_length, block_size)
    cos_table, sin_table = rope_tables(key_positions, HEAD_DIM)
    first_row = row_id * query_rows

    def query_part(array):
        if row_parts == 1:
            return array
        return lax.dynamic_slice_in_dim(array, first_row, query_rows, 0)

    query_cos, query_sin = query_part(cos_table), query_part(sin_table)
    row_positions = query_part(key_positions)

    inputs = tokens[0].astype(jnp.float32)
    normed_one = low(rms_norm(seq_tokens.astype(jnp.float32), gains[0]))
    normed_query = query_part(normed_one)
    queries = low(rotate(dot(normed_query, head_qkv[:, :HEAD_DIM]), query_cos, query_sin))
    kv_raw = dot(normed_one, head_qkv[:, HEAD_DIM:])
    kv_mine = low(jnp.where(core_id == 0, rotate(kv_raw, cos_table, sin_table), kv_raw))
    kv_other = exchange(kv_mine, "core")
    keys = jnp.where(core_id == 0, kv_mine, kv_other)
    values = jnp.where(core_id == 0, kv_other, kv_mine)
    attended, log_total = attend(queries, keys, values, row_positions, key_positions)
    branch = scatter_plane(head_terms(low(dot_t(attended, head_out))))
    hidden_in = after(inputs, own_gate_up, down_mine) + rms_norm(branch, gains[1])

    part_rows = row_count // 2

    def part(array, index):
        return array[index * part_rows : (index + 1) * part_rows]

    normed_two_mine = low(rms_norm(hidden_in, gains[2]))
    down_mine = after(down_mine, normed_two_mine)
    down_near = gather_plane_near(down_mine)
    upstream = cotangent[0].astype(jnp.float32)

    def forward_part(gate_up, own_down, zero):
        activated = low(gated_unit(gate_up[:, :ff_own], gate_up[:, ff_own:]))
        terms, _ = tensor_terms(low(dot_t(activated, own_down)), zero)
        return activated, terms, over_fsdp(terms, fsdp_count)

    def factors_of(gate_up, zero):
        gate_part, up_part = gate_up[:, :ff_own] + zero, gate_up[:, ff_own:] + zero
        _, pull_back = jax.vjp(gated_unit, gate_part, up_part)
        factors = pull_back(jnp.ones_like(gate_part))
        return lax.optimization_barrier(tuple(low(factor) for factor in factors))

    def turn_part(index, pieces, zero):
        lowered = jnp.sum(pieces.astype(jnp.float32), 0)
        output = low(part(hidden_in, index) + rms_norm(lowered, gains[3]))
        grad_lowered, gain = norm_back(lowered, gains[3], part(upstream, index))
        return output, low(grad_lowered + zero), gain

    def backward_part(grad_lowered, factors, zero, terms_zero):
        grad_activated = dot(grad_lowered, own_down) + zero
        grad_gate_up = lax.optimization_barrier(
            low(jnp.concatenate([grad_activated * factors[0], grad_activated * factors[1]], 1))
        )
        terms, sent = tensor_terms(low(dot_t(grad_gate_up, own_gate_up)), terms_zero)
        return grad_gate_up, terms, sent, over_fsdp(terms, fsdp_count)

    def both(first, second, zero=0.0):
        whole = jnp.concatenate(lax.optimization_barrier((first, second)), 0)
        return lax.optimization_barrier(whole + jnp.asarray(zero, whole.dtype))

    rows_one = gather_rows(part(normed_two_mine, 0), TENSOR)
    rows_two = gather_rows(part(normed_two_mine, 1), TENSOR)
    product_one = dot(rows_one, own_gate_up)
    own_down = gather_plane_far(down_mine, down_near, zero_after(product_one))
    if row_parts > 1:
        own_down = gather_rows(own_down, "row")
    activated_one, lowered_terms, pieces_one = forward_part(product_one, own_down, 0.0)
    output_one, sent_one, gain_three_one = turn_part(0, pieces_one, 0.0)
    lowered_one = gather_rows(sent_one, TENSOR)
    product_two = dot(after(rows_two, lowered_terms), own_gate_up)
    activated_two, lowered_terms, pieces_two = forward_part(
        product_two, own_down, zero_after(sent_one)
    )
    later = zero_after(lowered_terms)
    factors_one, factors_two = factors_of(product_one, later), factors_of(product_two, later)
    normed_two = both(rows_one, rows_two, later)
    activated = both(activated_one, activated_two, later)
    output_two, sent_two, gain_three_two = turn_part(
        1, pieces_two, zero_after(normed_two, activated, *factors_one, *factors_two)
    )
    lowered_two = gather_rows(sent_two, TENSOR)
    output = jnp.concatenate([output_one, output_two], 0)[None]
    gain_three = gain_three_one + gain_three_two
    gate_up_one, terms_one, _, back_one = backward_part(
        lowered_one, factors_one, zero_after(sent_two), 0.0
    )
    normed_two_one = jnp.sum(back_one.astype(jnp.float32), 0)
    grad_lowered = both(lowered_one, lowered_two, zero_after(terms_one))
    term_down = low(t_dot(grad_lowered, activated))
    gate_up_two, terms_two, halves_sent, back_two = backward_part(
        lowered_two, factors_two, zero_after(term_down), zero_after(normed_two_one)
    )

    plane_down = scatter_rows(term_down, ("row",) + PLANE)
    grad_gate_up = both(gate_up_one, gate_up_two)
    term_gate = low(t_dot(normed_two, after(grad_gate_up[:, :ff_own], halves_sent, normed_two_one)))
    plane_gate = scatter_rows(term_gate, ("row",) + PLANE)
    term_up = low(t_dot(normed_two, after(grad_gate_up[:, ff_own:], term_gate, terms_two)))
    plane_up = scatter_rows(term_up, ("row",) + PLANE)
    normed_two_two = jnp.sum(after(back_two, term_up).astype(jnp.float32), 0)
    grad_normed_two = jnp.concatenate([normed_two_one, normed_two_two], 0)

    grad_hidden_part, gain_two = norm_back(hidden_in, gains[2], grad_normed_two)
    grad_hidden = upstream + grad_hidden_part
    grad_branch, gain_one = norm_back(branch, gains[1], grad_hidden)
    grad_branch_mine = low(grad_branch)
    blocks_down = blocks_back(after(plane_down, grad_normed_two), TENSOR, tensor_parts)
    grad_branch = gather_heads(grad_branch_mine, blocks_down)
    blocks_gate = blocks_back(plane_gate, TENSOR, tensor_parts)

    grad_attended = low(dot(grad_branch, head_out))
    query_back, kv_terms, kv_sent = attend_back(
        core_id,
        queries,
        keys,
        values,
        grad_attended,
        log_total,
        row_positions,
        key_positions,
        query_cos,
        query_sin,
    )
    kv_terms = kv_terms + exchange(kv_sent, "core")
    if row_parts > 1:
        kv_terms = scatter_rows(kv_terms, "row")
    kv_back = jnp.where(core_id == 0, rotate(kv_terms, query_cos, -query_sin), kv_terms)
    grad_projected = jnp.concatenate([query_back, low(kv_back + zero_after(blocks_gate))], 1)
    grad_normed_one = scatter_plane(head_terms(low(dot_t(grad_projected, head_qkv))))
    grad_input_part, gain_zero = norm_back(inputs, gains[0], grad_normed_one)
    token_grad = low(grad_hidden + grad_input_part)[None]

    def to_owners(term):
        blocks = term.reshape(row_parts * HEADS * fsdp_count, -1, term.shape[1])
        return lax.all_to_all(blocks, EVERY, split_axis=0, concat_axis=0, tiled=True)

    def head_grad(pieces):
        pieces = pieces.reshape((row_parts, HEADS, fsdp_count) + pieces.shape[1:])
        return jnp.swapaxes(jnp.sum(pieces.astype(jnp.float32), (0, 2)), 0, 1)

    qkv_term = low(t_dot(normed_query, grad_projected))
    if row_parts > 1:
        qkv_term = scatter_rows(qkv_term, "row")
    by_owner = jnp.swapaxes(qkv_term.reshape(HEADS, fsdp_count, own_rows, -1), 0, 1)
    qkv_mine = scatter_rows(by_owner.reshape(qkv_term.shape), "fsdp")
    out_term = lax.optimization_barrier(low(t_dot(grad_branch, attended)))
    out_pieces = to_owners(out_term)
    blocks_up = blocks_back(after(plane_up, qkv_term), TENSOR, tensor_parts)
    qkv_blocks = blocks_back(qkv_mine, HEAD_AXES, HEADS)
    sum_qkv = jnp.swapaxes(qkv_blocks, 0, 1).astype(jnp.float32)
    gain_terms = jnp.stack([gain_zero, gain_one, gain_two, gain_three], 0)
    gain_terms = jnp.swapaxes(gain_terms.reshape(4, -1, own_rows), 0, 1)
    gain_pieces = lax.all_to_all(
        after(gain_terms, qkv_blocks), EVERY, split_axis=0, concat_axis=0, tiled=True
    )
    grad_gains = jnp.sum(gain_pieces, 0)
    grad_out = head_grad(out_pieces).reshape(own_rows, q_width)
    kv_sum = sum_qkv[:, :, HEAD_DIM:].reshape(own_rows, KV_HEADS, 2, HEAD_DIM)
    grad_qkv = jnp.concatenate(
        [
            sum_qkv[:, :, :HEAD_DIM].reshape(own_rows, q_width),
            kv_sum[:, :, 0].reshape(own_rows, kv_width),
            kv_sum[:, :, 1].reshape(own_rows, kv_width),
        ],
        1,
    )
    grad_down = side_by_side(blocks_down)
    grad_gate_up_w = jnp.concatenate(
        [after(side_by_side(blocks_gate), qkv_mine), side_by_side(blocks_up)], 1
    )
    moment_qkv, square_qkv, new_qkv = adamw(
        w_qkv, first_qkv, second_qkv, grad_qkv, MATRIX_RATE, WEIGHT_DECAY
    )
    moment_out, square_out, new_out = adamw(
        w_out, first_out, second_out, grad_out, MATRIX_RATE, WEIGHT_DECAY
    )
    moment_gate_up, square_gate_up, new_gate_up = adamw(
        w_gate_up, first_gate_up, second_gate_up, grad_gate_up_w, MATRIX_RATE, WEIGHT_DECAY
    )
    moment_down, square_down, new_down = adamw(
        w_down, first_down, second_down, grad_down, MATRIX_RATE, WEIGHT_DECAY
    )
    moment_gains, square_gains, new_gains = adamw(
        norm_gains, first_gains, second_gains, grad_gains, GAIN_RATE, 0.0
    )
    return (
        output,
        token_grad,
        moment_qkv,
        moment_out,
        moment_gate_up,
        moment_down,
        moment_gains,
        square_qkv,
        square_out,
        square_gate_up,
        square_down,
        square_gains,
        new_qkv,
        new_out,
        new_gate_up,
        new_down,
        new_gains,
    )


def solution(mesh):
    ctx_count, fsdp_count = mesh.shape["ctx"], mesh.shape["fsdp"]
    fine_mesh = Mesh(mesh.devices.reshape(ctx_count // HEADS, 2, 2, 2, fsdp_count), EVERY)
    rows = P("fsdp", CTX, None)
    weight = P(EVERY, None)
    gain = P(None, EVERY)
    weights = (weight, weight, weight, weight, gain)
    return jax.shard_map(
        per_device,
        mesh=fine_mesh,
        in_specs=(rows, rows, P()) + weights * 3,
        out_specs=(rows, rows) + weights * 3,
        check_vma=False,
    )
```
